32 devices in a mesh: section: 2 (over x), fsdp: 16 (over z, y, core).
Axes of the slice: x: 2, y: 2, z: 4, core: 2. Of those that a mesh axis runs over, the one named last changes fastest.
Arguments:
- section_inputs: bfloat16 [2, 2048, 1536], P('section', 'fsdp'), may hold values from -6 to 6
- seq_lengths: int32 [32, 4], P('fsdp'), may hold values from 1 to 61, as said below
- norm_gains: float32 [2, 2, 1536], replicated, may hold values from 0.25 to 1.75
- head_gains: float32 [2, 64], replicated, may hold values from 0.25 to 1.75
- conv_kernel: float32 [3, 1536], replicated, may hold values from -3 to 3
- first_weight: bfloat16 [2, 1536, 1536], P('section', 'fsdp'), may hold values from -0.15625 to 0.15625
- out_weight: bfloat16 [2, 1536, 1536], P('section', 'fsdp'), may hold values from -0.3125 to 0.3125
- gate_weight: bfloat16 [2, 1536, 6912], P('section', 'fsdp'), may hold values from -0.15625 to 0.15625
- up_weight: bfloat16 [2, 1536, 6912], P('section', 'fsdp'), may hold values from -0.15625 to 0.15625
- down_weight: bfloat16 [2, 6912, 1536], P('section', None, 'fsdp'), may hold values from -0.078125 to 0.078125
- pair_weight: bfloat16 [1536, 1024], P('fsdp'), may hold values from -0.15625 to 0.15625
- gating_weight: bfloat16 [1536, 3072], P('fsdp'), may hold values from -0.15625 to 0.15625
Outputs:
- activations: bfloat16 [2, 2048, 1536], P('section', 'fsdp')
- input_grads: bfloat16 [2, 2048, 1536], P('section', 'fsdp')
- grad_norm_gains: float32 [2, 2, 1536], replicated
- grad_head_gains: float32 [2, 64], replicated
- grad_conv_kernel: float32 [3, 1536], replicated
- grad_first: float32 [2, 1536, 1536], P('section', 'fsdp')
- grad_out: float32 [2, 1536, 1536], P('section', 'fsdp')
- grad_gate: float32 [2, 1536, 6912], P('section', 'fsdp')
- grad_up: float32 [2, 1536, 6912], P('section', 'fsdp')
- grad_down: float32 [2, 6912, 1536], P('section', None, 'fsdp')
- grad_pair: float32 [1536, 1024], P('fsdp')
- grad_gating: float32 [1536, 3072], P('fsdp')
The draws below stay inside these ranges and needn't reach their ends.
Inputs may be any that keep to these rules, and one draw needn't show every extreme that they name: `seq_lengths`: each row lists 4 sequence lengths whose sum lies between 16 and 64; some row sums to 64 and holds a sequence of the largest length.
All inputs are finite; a program needn't handle non-finite values.
Results may differ from the reference program's by a relative error of at most 0.025.
Values may be sent and summed in bfloat16 or wider, within the bound.
No kernel may reach another device: no remote copies, remote signals or barrier semaphores. Data moves between devices by JAX's collectives and lax.ppermute only.
A program may use at most 448 MiB of HBM per device.

```python
import jax
import jax.numpy as jnp
from jax import lax

D = 1536
FF = 6912
HEADS = 24
KV_HEADS = 8
HEAD_DIM = 64
TOK_MB = 64
SEQS = 4
TOKENS = 2048


def draw_seq_lengths(key, part):
    key = jax.random.fold_in(key, 11)
    total_key, cut_key = jax.random.split(key)
    row_total = TOKENS // TOK_MB
    totals = jax.random.randint(total_key, (row_total,), TOK_MB // 4, TOK_MB + 1)
    totals = totals.at[0].set(TOK_MB)
    cuts = jax.random.randint(cut_key, (row_total, SEQS - 1), 0, (totals - SEQS + 1)[:, None])
    cuts = jnp.sort(cuts, axis=-1)
    cuts = cuts.at[0].set(0)
    edges = jnp.concatenate([jnp.zeros((row_total, 1), jnp.int32), cuts, (totals - SEQS)[:, None]], axis=1)
    return (jnp.diff(edges, axis=1) + 1).astype(jnp.int32)


def block_levels(key, dims, shards, least, high):
    level = 1.0
    for dim, shards_of in shards:
        heights = jax.random.uniform(jax.random.fold_in(jax.random.fold_in(key, 6), dim), (shards_of,), jnp.float32, least / len(shards), high / len(shards))
        level = level * jnp.repeat(jnp.exp(heights), dims[dim] // shards_of).reshape((-1,) + (1,) * (len(dims) - 1 - dim))
    return level


def centred(rng, extent, spread, bound, cuts=(), held_as=jnp.bfloat16):
    loudness = block_levels(rng, extent, cuts, -0.22, 0.18) if cuts else 1.0
    values = jax.random.normal(rng, extent, jnp.float32) * spread * loudness
    return jnp.minimum(jnp.maximum(values, -bound), bound).astype(held_as)


def setup_inputs(seed: int = 0) -> dict:
    streams_of = jax.random.split(jax.random.key(seed), 13)
    return {
        "section_inputs": centred(streams_of[0], (2, TOKENS, D), 1.0, 6.0, ((0, 2), (1, 16))),
        "seq_lengths": draw_seq_lengths(jax.random.fold_in(streams_of[12], 71), 0),
        "norm_gains": jnp.clip(1.0 + 0.15 * jax.random.normal(streams_of[2], (2, 2, D), jnp.float32), 0.25, 1.75),
        "head_gains": jnp.clip(1.0 + 0.15 * jax.random.normal(streams_of[3], (2, HEAD_DIM), jnp.float32), 0.25, 1.75),
        "conv_kernel": centred(streams_of[4], (3, D), 0.6, 3.0, (), jnp.float32),
        "first_weight": centred(streams_of[5], (2, D, D), D ** -0.5, 0.15625, ((0, 2), (1, 16))),
        "out_weight": centred(streams_of[6], (2, D, D), (D // 4) ** -0.5, 0.3125, ((0, 2), (1, 16))),
        "gate_weight": centred(streams_of[7], (2, D, FF), D ** -0.5, 0.15625, ((0, 2), (1, 16))),
        "up_weight": centred(streams_of[8], (2, D, FF), D ** -0.5, 0.15625, ((0, 2), (1, 16))),
        "down_weight": centred(streams_of[9], (2, FF, D), FF ** -0.5, 0.078125, ((0, 2), (2, 16))),
        "pair_weight": centred(streams_of[10], (D, 2 * KV_HEADS * HEAD_DIM), D ** -0.5, 0.15625, ((0, 16),)),
        "gating_weight": centred(streams_of[11], (D, 2 * D), D ** -0.5, 0.15625, ((0, 16),)),
    }


EPSILON = 1e-05
ROPE_BASE = 1000000.0
MASKED_SCORE = -1000000000.0

@jax.custom_vjp
def low(v):
    return lax.optimization_barrier(v.astype(jnp.bfloat16)).astype(jnp.float32)

@jax.custom_vjp
def low_back(v):
    return v

def low_keep(v):
    return (low(v), None)

def low_pass(kept, grad):
    return (grad,)

def back_keep(v):
    return (v, None)

def back_low(kept, grad):
    return (low(grad),)
low.defvjp(low_keep, low_pass)
low_back.defvjp(back_keep, back_low)

def layout(lengths):
    seq_ends = jnp.cumsum(lengths, axis=-1)
    offsets = jnp.arange(TOK_MB, dtype=jnp.int32)
    passed = (offsets[:, None] >= seq_ends[..., None, :]).astype(jnp.int32)
    segments = lax.optimization_barrier(jnp.sum(passed, axis=-1))
    positions = offsets - lax.optimization_barrier(jnp.sum(passed * lengths[..., None, :], axis=-1))
    valid = segments < lengths.shape[-1]
    return (segments, positions, valid)

def norm_rows(values, scale_gain):
    return values * lax.rsqrt(lax.optimization_barrier(jnp.mean(values * values, axis=-1, keepdims=True)) + EPSILON) * scale_gain

def rotate(values, positions):
    half_width = values.shape[-1] // 2
    frequency = ROPE_BASE ** (-2.0 * jnp.arange(half_width, dtype=jnp.float32) / values.shape[-1])
    angles = positions.astype(jnp.float32)[..., None, None] * frequency
    cosine = jnp.cos(angles)
    sine_part = jnp.sin(angles)
    front_half = values[..., :half_width]
    back_half = values[..., half_width:]
    return jnp.concatenate([front_half * cosine - back_half * sine_part, back_half * cosine + front_half * sine_part], axis=-1)

def product(left_array, right_array):
    return jnp.matmul(left_array, right_array, precision=lax.Precision.HIGHEST)

def attention(normed, first_matrix, pair_matrix, head_gain_pair, segments, positions):
    buffers = normed.shape[0]
    row_count = normed.shape[1]
    group_size = HEADS // KV_HEADS
    queries = low_back(product(normed, first_matrix)).reshape(buffers, row_count, HEADS, HEAD_DIM)
    key_values = low_back(product(normed, pair_matrix)).reshape(buffers, row_count, 2, KV_HEADS, HEAD_DIM)
    queries_rot = low(rotate(norm_rows(queries, head_gain_pair[0]), positions))
    queries_rot = queries_rot.reshape(buffers, row_count, KV_HEADS, group_size, HEAD_DIM)
    keys_rot = low(rotate(norm_rows(key_values[:, :, 0], head_gain_pair[1]), positions))
    values = low(key_values[:, :, 1])
    offsets = jnp.arange(row_count)
    allowed = (segments[:, :, None] == segments[:, None, :]) & (offsets[:, None] >= offsets[None, :])[None]
    scale_factor = HEAD_DIM ** (-0.5)
    scores = jnp.einsum('bqhgd,bkhd->bhgqk', queries_rot, keys_rot, precision=lax.Precision.HIGHEST) * scale_factor
    scores = low_back(jnp.where(allowed[:, None, None], scores, MASKED_SCORE))
    probabilities = low(jax.nn.softmax(scores, axis=-1))
    mixed = jnp.einsum('bhgqk,bkhd->bqhgd', probabilities, values, precision=lax.Precision.HIGHEST)
    return low_back(low(mixed.reshape(buffers, row_count, HEADS * HEAD_DIM)))

def convolve(normed, first_matrix, gating_matrix, kernel_rows, positions):
    row_count = normed.shape[1]
    model_width = first_matrix.shape[1]
    signal = low_back(product(normed, first_matrix))
    gate_pair = low_back(product(normed, gating_matrix))
    carried = gate_pair[..., :model_width] * signal
    summed = kernel_rows[0] * carried
    for lag_steps in (1, 2):
        delayed = jnp.pad(carried, ((0, 0), (lag_steps, 0), (0, 0)))[:, :row_count]
        summed = summed + kernel_rows[lag_steps] * jnp.where((positions >= lag_steps)[..., None], delayed, 0.0)
    return low(gate_pair[..., model_width:] * summed)

def block(block_input, block_gains, first_matrix, out_matrix, gate_matrix, up_matrix, down_matrix, mixer_fn):
    normed = low(norm_rows(block_input, block_gains[0]))
    hidden = block_input + low_back(product(mixer_fn(normed, first_matrix), out_matrix))
    normed_h = low(norm_rows(hidden, block_gains[1]))
    gate_pre = low_back(product(normed_h, gate_matrix))
    up_pre = low_back(product(normed_h, up_matrix))
    active = low(jax.nn.silu(gate_pre) * up_pre)
    return hidden + low_back(product(active, down_matrix))

def reference(section_inputs, seq_lengths, norm_gains, head_gains, conv_kernel, first_weight, out_weight, gate_weight, up_weight, down_weight, pair_weight, gating_weight):
    buffers = TOKENS // TOK_MB
    segments, positions, valid = layout(seq_lengths)
    start_rows = section_inputs[0].astype(jnp.float32).reshape(buffers, TOK_MB, D)
    cotangent = section_inputs[1].astype(jnp.float32).reshape(buffers, TOK_MB, D)
    cotangent = jnp.where(valid[..., None], cotangent, 0.0)
    shift_rows = jnp.zeros((buffers, TOK_MB, D), jnp.float32)

    def forward(start_in, shift_in, gains_in, heads_in, kernel_in, first_in, out_in, gate_in, up_in, down_in, pair_in, gating_in):

        def attend(normed, first_matrix):
            return attention(normed, first_matrix, pair_in, heads_in, segments, positions)

        def mixing(normed, first_matrix):
            return convolve(normed, first_matrix, gating_in, kernel_in, positions)
        middle = block(start_in, gains_in[0], first_in[0], out_in[0], gate_in[0], up_in[0], down_in[0], attend)
        sent_rows = low_back(low(middle) + shift_in)
        final_rows = block(sent_rows, gains_in[1], first_in[1], out_in[1], gate_in[1], up_in[1], down_in[1], mixing)
        return (final_rows, middle)
    primals = (start_rows, shift_rows, norm_gains.astype(jnp.float32), head_gains.astype(jnp.float32), conv_kernel.astype(jnp.float32), first_weight.astype(jnp.float32), out_weight.astype(jnp.float32), gate_weight.astype(jnp.float32), up_weight.astype(jnp.float32), down_weight.astype(jnp.float32), pair_weight.astype(jnp.float32), gating_weight.astype(jnp.float32))
    final_rows, pull_back, middle = jax.vjp(forward, *primals, has_aux=True)
    grads = pull_back(cotangent)
    stacked = jnp.where(valid[None, ..., None], jnp.stack([middle, final_rows]), 0.0)
    activations = stacked.astype(jnp.bfloat16).reshape(2, TOKENS, D)
    input_grads = jnp.stack([grads[0], grads[1]]).astype(jnp.bfloat16).reshape(2, TOKENS, D)
    return (activations, input_grads, grads[2], grads[3], grads[4], grads[5], grads[6], grads[7], grads[8], grads[9], grads[10], grads[11])
```

```python
import jax
import jax.numpy as jnp
from jax import lax
from jax.sharding import PartitionSpec as P

HEADS = 24
KV_HEADS = 8
HEAD_DIM = 64
TOK_MB = 64
SIDES = 2
GROUP = 16
CHIPS = 8
RING = (0, 2, 4, 6, 7, 5, 3, 1)

EPSILON = 1e-05
ROPE_BASE = 1000000.0
MASKED_SCORE = -1000000000.0

BF = jnp.bfloat16
F32 = jnp.float32


def group_pairs(chip_pairs, outer):
    return [
        (GROUP * o + 2 * a + c, GROUP * o + 2 * b + c)
        for o in range(outer)
        for a, b in chip_pairs
        for c in range(2)
    ]


def forward_ring(outer):
    return group_pairs([(RING[i], RING[(i + 1) % CHIPS]) for i in range(CHIPS)], outer)


def backward_ring(outer):
    return group_pairs([(RING[(i + 1) % CHIPS], RING[i]) for i in range(CHIPS)], outer)


def other_core(value, outer):
    return lax.ppermute(value, "fsdp", [(i, i ^ 1) for i in range(GROUP * outer)])


def other_side(value):
    return lax.ppermute(value, "section", [(0, 1), (1, 0)])


def to_side(value, side):
    return lax.ppermute(value, "section", [(1 - side, side)])


def ring_gather(own, outer):
    fwd, bwd = forward_ring(outer), backward_ring(outer)
    blocks = [own]
    up, down = own, own
    for _ in range(3):
        up, down = lax.ppermute(up, "fsdp", fwd), lax.ppermute(down, "fsdp", bwd)
        blocks += [up, down]
    half = own.shape[1] // 2
    left = lax.ppermute(up[:, :half], "fsdp", fwd)
    right = lax.ppermute(down[:, half:], "fsdp", bwd)
    blocks.append(jnp.concatenate([left, right], axis=1))
    return jnp.concatenate(blocks, axis=0)


def ring_scatter(terms, outer):
    fwd, bwd = forward_ring(outer), backward_ring(outer)
    rows = terms.shape[0] // CHIPS
    half = terms.shape[1] // 2
    block = {
        d: terms[i * rows : (i + 1) * rows] for i, d in enumerate((0, -1, 1, -2, 2, -3, 3, 4))
    }
    up = lax.ppermute(block[4][:, :half].astype(BF), "fsdp", fwd).astype(F32)
    down = lax.ppermute(block[4][:, half:].astype(BF), "fsdp", bwd).astype(F32)
    up = jnp.concatenate([block[3][:, :half] + up, block[3][:, half:]], axis=1)
    down = jnp.concatenate([block[-3][:, :half], block[-3][:, half:] + down], axis=1)
    for step in (2, 1, 0):
        up = lax.ppermute(up.astype(BF), "fsdp", fwd).astype(F32)
        down = lax.ppermute(down.astype(BF), "fsdp", bwd).astype(F32)
        if step:
            up = block[step] + up
            down = block[-step] + down
    return block[0] + up + down


def layout(lengths):
    seq_ends = jnp.cumsum(lengths, axis=-1)
    offsets = jnp.arange(TOK_MB, dtype=jnp.int32)
    passed = (offsets[:, None] >= seq_ends[..., None, :]).astype(jnp.int32)
    segments = jnp.sum(passed, axis=-1)
    positions = offsets - jnp.sum(passed * lengths[..., None, :], axis=-1)
    valid = segments < lengths.shape[-1]
    return (segments, positions, valid)


def norm_rows(values, scale_gain):
    return (
        values * lax.rsqrt(jnp.mean(values * values, axis=-1, keepdims=True) + EPSILON) * scale_gain
    )


def rotate(values, positions):
    half_width = values.shape[-1] // 2
    frequency = ROPE_BASE ** (-2.0 * jnp.arange(half_width, dtype=F32) / values.shape[-1])
    angles = positions.astype(F32)[..., None, None] * frequency
    cosine = jnp.cos(angles)
    sine_part = jnp.sin(angles)
    front_half = values[..., :half_width]
    back_half = values[..., half_width:]
    return jnp.concatenate(
        [front_half * cosine - back_half * sine_part, back_half * cosine + front_half * sine_part],
        axis=-1,
    )


def forward_dot(left_array, right_array):
    return jnp.dot(left_array, right_array, preferred_element_type=F32)


def back_dot(grad_array, weight_array):
    return lax.dot_general(
        grad_array, weight_array, (((1,), (1,)), ((), ())), preferred_element_type=F32
    )


def row_outer(left_array, right_array):
    return lax.dot_general(
        left_array, right_array, (((0,), (0,)), ((), ())), preferred_element_type=F32
    )


def prepare(queries, keys_in, head_gain_pair, positions):
    return (
        rotate(norm_rows(queries, head_gain_pair[0]), positions),
        rotate(norm_rows(keys_in, head_gain_pair[1]), positions),
    )


def attention_parts(normed, first_matrix, pair_matrix, head_gain_pair, segments, positions):
    row_count = normed.shape[0]
    kv_heads = KV_HEADS // SIDES
    group_size = HEADS // KV_HEADS
    queries = forward_dot(normed, first_matrix).reshape(row_count, HEADS // SIDES, HEAD_DIM)
    key_values = forward_dot(normed, pair_matrix).reshape(row_count, 2, kv_heads, HEAD_DIM)
    queries_rot, keys_rot = prepare(queries, key_values[:, 0], head_gain_pair, positions)
    queries_low = queries_rot.astype(BF).reshape(row_count, kv_heads, group_size, HEAD_DIM)
    keys_low = keys_rot.astype(BF)
    values_low = key_values[:, 1].astype(BF)
    offsets = jnp.arange(row_count)
    allowed = (segments[:, None] == segments[None, :]) & (offsets[:, None] >= offsets[None, :])
    scale_factor = HEAD_DIM ** (-0.5)
    scores = (
        jnp.einsum("qhgd,khd->hgqk", queries_low, keys_low, preferred_element_type=F32)
        * scale_factor
    )
    scores = jnp.where(allowed, scores, MASKED_SCORE)
    probabilities = jax.nn.softmax(scores, axis=-1)
    probs_low = probabilities.astype(BF)
    mixed = jnp.einsum("hgqk,khd->qhgd", probs_low, values_low, preferred_element_type=F32)
    mixed = mixed.reshape(row_count, -1).astype(BF)
    return (
        mixed,
        (queries, key_values, queries_low, keys_low, values_low, probabilities, probs_low),
    )


def attention_back(grad_out, context, first_matrix, pair_matrix, head_gain_pair, positions):
    queries, key_values, queries_low, keys_low, values_low, probabilities, probs_low = context
    row_count = grad_out.shape[0]
    kv_heads = KV_HEADS // SIDES
    group_size = HEADS // KV_HEADS
    scale_factor = HEAD_DIM ** (-0.5)
    grad_low = grad_out.astype(BF).reshape(row_count, kv_heads, group_size, HEAD_DIM)
    grad_probs = jnp.einsum("qhgd,khd->hgqk", grad_low, values_low, preferred_element_type=F32)
    grad_values = jnp.einsum("hgqk,qhgd->khd", probs_low, grad_low, preferred_element_type=F32)
    grad_scores = probabilities * (
        grad_probs - jnp.sum(grad_probs * probabilities, axis=-1, keepdims=True)
    )
    grad_scores = grad_scores.astype(BF)
    grad_queries = (
        jnp.einsum("hgqk,khd->qhgd", grad_scores, keys_low, preferred_element_type=F32)
        * scale_factor
    )
    grad_keys = (
        jnp.einsum("hgqk,qhgd->khd", grad_scores, queries_low, preferred_element_type=F32)
        * scale_factor
    )

    def prepared(query_in, key_in, gain_in):
        return prepare(query_in, key_in, gain_in, positions)

    unused_value, pull_prep = jax.vjp(prepared, queries, key_values[:, 0], head_gain_pair)
    grad_query_pre, grad_key_pre, grad_head = pull_prep(
        (grad_queries.reshape(queries.shape), grad_keys)
    )
    grad_first = grad_query_pre.reshape(row_count, -1).astype(BF)
    grad_pairs = (
        jnp.stack([grad_key_pre, grad_values], axis=1).reshape(row_count, -1).astype(BF)
    )
    grad_normed = back_dot(grad_first, first_matrix) + back_dot(grad_pairs, pair_matrix)
    return (grad_normed, grad_first, grad_pairs, grad_head)


def conv_mix(signal, gate_pair, kernel_rows, positions):
    width = signal.shape[-1]
    carried = gate_pair[:, :width] * signal
    summed = kernel_rows[0] * carried
    for lag_steps in (1, 2):
        delayed = jnp.concatenate(
            [jnp.zeros((lag_steps, width), F32), carried[:-lag_steps]], axis=0
        )
        summed = summed + kernel_rows[lag_steps] * jnp.where(
            (positions >= lag_steps)[:, None], delayed, 0.0
        )
    return gate_pair[:, width:] * summed


def conv_parts(normed, first_matrix, gating_matrix, kernel_rows, positions):
    signal = forward_dot(normed, first_matrix)
    gate_pair = forward_dot(normed, gating_matrix)
    mixed = conv_mix(signal, gate_pair, kernel_rows, positions).astype(BF)
    return (mixed, (signal, gate_pair))


def conv_back(grad_out, context, first_matrix, gating_matrix, kernel_rows, positions):
    signal, gate_pair = context

    def mixing(signal_in, gates_in, kernel_in):
        return conv_mix(signal_in, gates_in, kernel_in, positions)

    unused_value, pull_conv = jax.vjp(mixing, signal, gate_pair, kernel_rows)
    grad_signal, grad_gates, grad_kernel = pull_conv(grad_out)
    grad_first = grad_signal.astype(BF)
    grad_gates = grad_gates.astype(BF)
    grad_normed = back_dot(grad_first, first_matrix) + back_dot(grad_gates, gating_matrix)
    return (grad_normed, grad_first, grad_gates, grad_kernel)


def glu_unit(gate_in, up_in):
    return jax.nn.silu(gate_in) * up_in


def block_forward(start_rows, block_gains, run_mixer, out_half, mlp, outer):
    rows = start_rows.shape[0]
    normed = norm_rows(start_rows, block_gains[0]).astype(BF)
    normed_pair = jnp.concatenate([normed, other_side(normed)], axis=0)
    mixed, context = run_mixer(normed_pair)
    mixed_term = forward_dot(mixed, out_half)
    hidden = start_rows + mixed_term[:rows] + other_side(mixed_term[rows:].astype(BF)).astype(F32)
    normed_h = norm_rows(hidden, block_gains[1]).astype(BF)
    all_h = ring_gather(normed_h, outer)
    gate_pre = forward_dot(all_h, mlp[0])
    up_pre = forward_dot(all_h, mlp[1])
    active = glu_unit(gate_pre, up_pre).astype(BF)
    result = hidden + ring_scatter(back_dot(active, mlp[2]), outer)
    return (result, (start_rows, normed_pair, mixed, context, hidden, all_h, gate_pre, up_pre, active))


def block_backward(upstream, saved, block_gains, back_mixer, out_half, mlp, outer):
    start_rows, normed_pair, mixed, context, hidden, all_h, gate_pre, up_pre, active = saved
    rows = start_rows.shape[0]
    all_up = ring_gather(upstream, outer)
    grad_active = forward_dot(all_up, mlp[2])
    unused_value, pull_glu = jax.vjp(glu_unit, gate_pre, up_pre)
    grad_gate, grad_up = pull_glu(grad_active)
    grad_gate = grad_gate.astype(BF)
    grad_up = grad_up.astype(BF)
    grad_normed_h = ring_scatter(back_dot(grad_gate, mlp[0]) + back_dot(grad_up, mlp[1]), outer)
    mlp_terms = (
        row_outer(all_h, grad_gate),
        row_outer(all_h, grad_up),
        row_outer(all_up, active),
    )
    unused_norm, pull_hidden = jax.vjp(norm_rows, hidden, block_gains[1])
    grad_hidden, grad_gain_h = pull_hidden(grad_normed_h)
    grad_hidden = grad_hidden + upstream.astype(F32)
    grad_mixed = grad_hidden.astype(BF)
    grad_pair = jnp.concatenate([grad_mixed, other_side(grad_mixed)], axis=0)
    grad_normed, grad_first, grad_second, grad_small = back_mixer(
        back_dot(grad_pair, out_half), context
    )
    grad_normed = grad_normed[:rows] + other_side(grad_normed[rows:].astype(BF)).astype(F32)
    unused_start, pull_start = jax.vjp(norm_rows, start_rows, block_gains[0])
    grad_start, grad_gain_x = pull_start(grad_normed)
    grad_start = (grad_start + grad_hidden).astype(BF)
    mixer_terms = (
        row_outer(normed_pair, grad_first),
        row_outer(normed_pair, grad_second),
        row_outer(mixed, grad_pair),
    )
    return (grad_start, mlp_terms, mixer_terms, jnp.stack([grad_gain_x, grad_gain_h]), grad_small)


def on_device(
    section_inputs,
    seq_lengths,
    norm_gains,
    head_gains,
    conv_kernel,
    first_weight,
    out_weight,
    gate_weight,
    up_weight,
    down_weight,
    pair_weight,
    gating_weight,
):
    side = lax.axis_index("section")
    on_first = side == 0
    shards = lax.axis_size("fsdp")
    outer = shards // GROUP
    place = lax.axis_index("fsdp")
    core = place % 2
    on_core0 = core == 0
    same_core = [
        [GROUP * o + 2 * a + c for a in range(CHIPS)] for o in range(outer) for c in range(2)
    ]
    across = [[GROUP * o + i for o in range(outer)] for i in range(GROUP)]
    depth = first_weight.shape[1]
    model_width = first_weight.shape[2]
    half_width = model_width // SIDES
    pair_half = pair_weight.shape[1] // 2 // SIDES
    hidden_part = gate_weight.shape[2] // CHIPS

    def pick(first_value, second_value):
        return jnp.where(on_first, first_value, second_value)

    def half_of(columns, width):
        return lax.dynamic_slice_in_dim(columns, side * width, width, axis=1)

    def other_half_of(columns, width):
        return lax.dynamic_slice_in_dim(columns, (1 - side) * width, width, axis=1)

    rows = section_inputs[0]
    arrived = other_side(pick(rows[TOK_MB:], rows[:TOK_MB]))
    start_rows = pick(rows[:TOK_MB], arrived).astype(F32)
    cotangent = pick(arrived, rows[TOK_MB:])
    segments, positions, valid = layout(seq_lengths)
    own_valid = pick(valid[0], valid[1])[:, None]
    segments = segments + 8 * jnp.arange(2, dtype=jnp.int32)[:, None]
    segments = pick(segments.reshape(-1), segments[::-1].reshape(-1))
    positions = pick(positions.reshape(-1), positions[::-1].reshape(-1))

    first_own = half_of(first_weight[0], half_width)
    first_got = other_side(other_half_of(first_weight[0], half_width))
    pair_own = jnp.concatenate(
        [
            half_of(pair_weight[:, : pair_half * SIDES], pair_half),
            half_of(pair_weight[:, pair_half * SIDES :], pair_half),
        ],
        axis=1,
    )
    gating_own = jnp.concatenate(
        [
            half_of(gating_weight[:, :model_width], half_width),
            half_of(gating_weight[:, model_width:], half_width),
        ],
        axis=1,
    )
    low_place = place < shards // 2
    out_pairs = [(j, shards + j - shards // 2) for j in range(shards // 2, shards)] + [
        (shards + j, j + shards // 2) for j in range(shards // 2)
    ]
    out_back = [(b, a) for a, b in out_pairs]
    out_stays = on_first == low_place
    out_got = lax.ppermute(out_weight[0], ("section", "fsdp"), out_pairs)
    out_own = jnp.where(out_stays, out_weight[0], out_got)

    def whole(part):
        return lax.all_gather(part, "fsdp", axis=0, tiled=True)

    attention_in = whole(jnp.concatenate([pick(first_own, first_got), pair_own], axis=1))
    out_both = whole(out_own)
    conv_in = whole(jnp.concatenate([pick(first_got, first_own), gating_own], axis=1))
    first_halves = (attention_in[:, :half_width], conv_in[:, :half_width])
    pair_part = attention_in[:, half_width:]
    gating_part = conv_in[:, half_width:]
    out_halves = (out_both[:half_width], out_both[half_width:])

    def spread(matrix):
        if outer > 1:
            matrix = lax.all_gather(
                matrix, "fsdp", axis=0, tiled=True, axis_index_groups=across
            )
        return matrix.reshape(-1, CHIPS, hidden_part).transpose(1, 0, 2)

    local = jnp.stack(
        [spread(gate_weight[0]), spread(up_weight[0]), spread(down_weight[0].T)], axis=1
    )
    local = lax.all_to_all(local, "fsdp", 0, 0, axis_index_groups=same_core)
    crossed = other_side(local)
    local_twin = other_core(local, outer)
    crossed_twin = other_core(crossed, outer)

    def assembled(number):
        mine = jnp.where(side == number, local, crossed)
        twin = jnp.where(side == number, local_twin, crossed_twin)
        both = jnp.stack(
            [jnp.where(on_core0, mine, twin), jnp.where(on_core0, twin, mine)], axis=1
        )
        both = both.reshape(CHIPS, 2, 3, outer, depth, hidden_part)
        both = both.transpose(2, 3, 0, 1, 4, 5).reshape(3, model_width, hidden_part)
        return (both[0], both[1], both[2])

    mlps = (assembled(0), assembled(1))

    def run_attention(normed):
        return attention_parts(
            normed, first_halves[0], pair_part, head_gains, segments, positions
        )

    def pull_attention(grad_out, context):
        return attention_back(
            grad_out, context, first_halves[0], pair_part, head_gains, positions
        )

    kernel_half = half_of(conv_kernel, half_width)

    def run_conv(normed):
        return conv_parts(normed, first_halves[1], gating_part, kernel_half, positions)

    def pull_conv(grad_out, context):
        return conv_back(
            grad_out, context, first_halves[1], gating_part, kernel_half, positions
        )

    middle, saved0 = block_forward(
        start_rows, norm_gains[0], run_attention, out_halves[0], mlps[0], outer
    )
    middle = middle.astype(BF)
    final, saved1 = block_forward(
        middle.astype(F32), norm_gains[1], run_conv, out_halves[1], mlps[1], outer
    )
    final = final.astype(BF)
    nothing = jnp.zeros_like(cotangent)
    grad_middle, mlp_terms1, mixer_terms1, gain_terms1, grad_kernel = block_backward(
        jnp.where(own_valid, cotangent, nothing),
        saved1,
        norm_gains[1],
        pull_conv,
        out_halves[1],
        mlps[1],
        outer,
    )
    grad_start, mlp_terms0, mixer_terms0, gain_terms0, grad_head = block_backward(
        grad_middle, saved0, norm_gains[0], pull_attention, out_halves[0], mlps[0], outer
    )

    def returned(first_rows, second_rows):
        kept = pick(first_rows, second_rows)
        came = other_side(pick(second_rows, first_rows))
        return jnp.concatenate([pick(kept, came), pick(came, kept)], axis=0)

    activation_rows = returned(
        jnp.where(own_valid, middle, nothing), jnp.where(own_valid, final, nothing)
    )
    input_rows = returned(grad_start, grad_middle)

    def section_sum(terms, number):
        stacked = jnp.stack([term.astype(BF) for term in terms], axis=0)
        stacked = stacked.reshape(3, outer, CHIPS, 2, depth, hidden_part)
        mine = lax.dynamic_index_in_dim(stacked, core, 3, keepdims=False)
        twin = lax.dynamic_index_in_dim(stacked, 1 - core, 3, keepdims=False)
        total = (mine.astype(F32) + other_core(twin, outer).astype(F32)).astype(BF)
        return (total.astype(F32) + to_side(total, number).astype(F32)).astype(BF)

    hidden_terms = pick(section_sum(mlp_terms0, 0), section_sum(mlp_terms1, 1))
    hidden_terms = hidden_terms.transpose(2, 0, 1, 3, 4)
    hidden_terms = lax.all_to_all(hidden_terms, "fsdp", 0, 0, axis_index_groups=same_core)
    if outer > 1:
        hidden_sums = lax.psum_scatter(
            hidden_terms, "fsdp", scatter_dimension=2, tiled=True, axis_index_groups=across
        )
    else:
        hidden_sums = hidden_terms
    hidden_sums = hidden_sums.reshape(CHIPS, 3, depth, hidden_part)
    hidden_sums = hidden_sums.transpose(1, 2, 0, 3).reshape(3, depth, -1).astype(F32)

    def scattered(term):
        return lax.psum_scatter(term.astype(BF), "fsdp", scatter_dimension=0, tiled=True)

    conv_sums = scattered(jnp.concatenate([mixer_terms1[0], mixer_terms1[1]], axis=1))
    attention_sums = scattered(jnp.concatenate([mixer_terms0[0], mixer_terms0[1]], axis=1))
    out_sums = scattered(jnp.concatenate([mixer_terms0[2], mixer_terms1[2]], axis=0))
    out_came = lax.ppermute(out_sums, ("section", "fsdp"), out_back)
    out_rows = jnp.where(out_stays, out_sums, out_came).astype(F32)

    def both_halves(own_part, came_part):
        return jnp.concatenate([pick(own_part, came_part), pick(came_part, own_part)], axis=1)

    sums = (attention_sums[:, :half_width], conv_sums[:, :half_width])
    first_rows = both_halves(pick(sums[0], sums[1]), other_side(pick(sums[1], sums[0])))
    second_parts = jnp.concatenate([attention_sums[:, half_width:], conv_sums[:, half_width:]], axis=1)
    second_came = other_side(second_parts)

    def columns(start, width):
        return both_halves(second_parts[:, start : start + width], second_came[:, start : start + width])

    pair_rows = jnp.concatenate([columns(0, pair_half), columns(pair_half, pair_half)], axis=1)
    gating_rows = jnp.concatenate(
        [columns(2 * pair_half, half_width), columns(2 * pair_half + half_width, half_width)], axis=1
    )

    kernel_whole = lax.dynamic_update_slice_in_dim(
        jnp.zeros_like(conv_kernel), grad_kernel, side * half_width, axis=1
    )
    small_sums = lax.psum(
        (jnp.stack([gain_terms0, gain_terms1]), grad_head, kernel_whole), ("section", "fsdp")
    )
    return (
        activation_rows[None],
        input_rows[None],
        small_sums[0],
        small_sums[1],
        small_sums[2],
        first_rows.astype(F32)[None],
        out_rows[None],
        hidden_sums[0][None],
        hidden_sums[1][None],
        hidden_sums[2].T[None],
        pair_rows.astype(F32),
        gating_rows.astype(F32),
    )


def solution(mesh):
    in_specs = (
        P("section", "fsdp", None),
        P("fsdp", None),
        P(),
        P(),
        P(),
        P("section", "fsdp", None),
        P("section", "fsdp", None),
        P("section", "fsdp", None),
        P("section", "fsdp", None),
        P("section", None, "fsdp"),
        P("fsdp", None),
        P("fsdp", None),
    )
    out_specs = (
        P("section", "fsdp", None),
        P("section", "fsdp", None),
        P(),
        P(),
        P(),
        P("section", "fsdp", None),
        P("section", "fsdp", None),
        P("section", "fsdp", None),
        P("section", "fsdp", None),
        P("section", None, "fsdp"),
        P("fsdp", None),
        P("fsdp", None),
    )
    return jax.shard_map(
        on_device, mesh=mesh, in_specs=in_specs, out_specs=out_specs, check_vma=False
    )
```

```python
import jax
import jax.numpy as jnp
from jax import lax
from jax.experimental import pallas as pl
from jax.experimental.pallas import tpu as pltpu
from jax.sharding import PartitionSpec as P

HEADS = 24
KV_HEADS = 8
HEAD_DIM = 64
TOK_MB = 64
SIDES = 2
GROUP = 16
CHIPS = 8
RING = (0, 2, 4, 6, 7, 5, 3, 1)

EPSILON = 1e-05
ROPE_BASE = 1000000.0
MASKED_SCORE = -1000000000.0

BF = jnp.bfloat16
F32 = jnp.float32


def group_pairs(chip_pairs, outer):
    return [
        (GROUP * o + 2 * a + c, GROUP * o + 2 * b + c)
        for o in range(outer)
        for a, b in chip_pairs
        for c in range(2)
    ]


def forward_ring(outer):
    return group_pairs([(RING[i], RING[(i + 1) % CHIPS]) for i in range(CHIPS)], outer)


def backward_ring(outer):
    return group_pairs([(RING[(i + 1) % CHIPS], RING[i]) for i in range(CHIPS)], outer)


def other_core(value, outer):
    return lax.ppermute(value, "fsdp", [(i, i ^ 1) for i in range(GROUP * outer)])


def other_side(value):
    return lax.ppermute(value, "section", [(0, 1), (1, 0)])


def to_side(value, side):
    return lax.ppermute(value, "section", [(1 - side, side)])


ORDER = (0, -1, 1, -2, 2, -3, 3, 4)


def ring_blocks(own, outer):
    fwd, bwd = forward_ring(outer), backward_ring(outer)
    blocks = [own]
    up, down = own, own
    for _ in range(3):
        up, down = lax.ppermute(up, "fsdp", fwd), lax.ppermute(down, "fsdp", bwd)
        blocks += [up, down]
    half = own.shape[1] // 2
    left = lax.ppermute(up[:, :half], "fsdp", fwd)
    right = lax.ppermute(down[:, half:], "fsdp", bwd)
    blocks.append(jnp.concatenate([left, right], axis=1))
    return blocks


def ring_gather(own, outer):
    return jnp.concatenate(ring_blocks(own, outer), axis=0)


class RingSum:
    def __init__(self, blocks, outer):
        self.ways = forward_ring(outer), backward_ring(outer)
        self.block = dict(zip(ORDER, blocks))
        self.half = blocks[0].shape[1] // 2
        self.sums = (self.block[4][:, : self.half], self.block[4][:, self.half :])
        self.left = 3

    def step(self, *values):
        up, down = (
            lax.ppermute(v.astype(BF), "fsdp", way) for v, way in zip(self.sums, self.ways)
        )
        up, down, values = pinned(up, down, values)
        up, down = up.astype(F32), down.astype(F32)
        block, half, left = self.block, self.half, self.left
        if left == 3:
            up = jnp.concatenate([block[3][:, :half] + up, block[3][:, half:]], axis=1)
            down = jnp.concatenate([block[-3][:, :half], block[-3][:, half:] + down], axis=1)
        elif left:
            up, down = block[left] + up, block[-left] + down
        self.sums = (up, down)
        self.left -= 1
        return values

    def total(self):
        while self.left >= 0:
            self.step()
        return self.block[0] + self.sums[0] + self.sums[1]


def ring_scatter(terms, outer, beside=()):
    rows = terms.shape[0] // CHIPS
    ring = RingSum([terms[i * rows : (i + 1) * rows] for i in range(CHIPS)], outer)
    beside = [ring.step(value)[0] for value in beside]
    return ring.total(), beside


def ring_chips(chip):
    odd = chip & 1
    spot = (chip >> 1) * (1 - 2 * odd) + 7 * odd
    spots = [(spot + d) & 7 for d in ORDER]
    return [2 * at + (at >> 2) * (15 - 4 * at) for at in spots]


def chip_sum(terms, place, outer):
    blocks = [
        sum(lax.dynamic_index_in_dim(t, chip, 0, keepdims=False).astype(F32) for t in terms)
        for chip in ring_chips(place // 2)
    ]
    return RingSum(blocks, outer)


class Scattered:
    def __init__(self, rows):
        self.rows = rows

    def step(self, *values):
        return values

    def total(self):
        return self.rows


def everywhere(value):
    value = value + other_side(value)
    for bit in range((lax.axis_size("fsdp") - 1).bit_length()):
        pairs = [(i, i ^ (1 << bit)) for i in range(lax.axis_size("fsdp"))]
        value = value + lax.ppermute(value, "fsdp", pairs)
    return value


def pinned(*values):
    return lax.optimization_barrier(values)


def layout(lengths):
    seq_ends = jnp.cumsum(lengths, axis=-1)
    offsets = jnp.arange(TOK_MB, dtype=jnp.int32)
    passed = (offsets[:, None] >= seq_ends[..., None, :]).astype(jnp.int32)
    segments = jnp.sum(passed, axis=-1)
    positions = offsets - jnp.sum(passed * lengths[..., None, :], axis=-1)
    valid = segments < lengths.shape[-1]
    return (segments, positions, valid)


def norm_rows(values, scale_gain):
    return (
        values * lax.rsqrt(jnp.mean(values * values, axis=-1, keepdims=True) + EPSILON) * scale_gain
    )


def rotate(values, positions):
    half_width = values.shape[-1] // 2
    frequency = ROPE_BASE ** (-2.0 * jnp.arange(half_width, dtype=F32) / values.shape[-1])
    angles = positions.astype(F32)[..., None, None] * frequency
    cosine = jnp.cos(angles)
    sine_part = jnp.sin(angles)
    front_half = values[..., :half_width]
    back_half = values[..., half_width:]
    return jnp.concatenate(
        [front_half * cosine - back_half * sine_part, back_half * cosine + front_half * sine_part],
        axis=-1,
    )


def forward_dot(left_array, right_array):
    return jnp.dot(left_array, right_array, preferred_element_type=F32)


def back_dot(grad_array, weight_array):
    return lax.dot_general(
        grad_array, weight_array, (((1,), (1,)), ((), ())), preferred_element_type=F32
    )


def outer_kernel(left_ref, right_ref, out_ref):
    out_ref[...] = lax.dot_general(
        left_ref[...], right_ref[...], (((0,), (0,)), ((), ())), preferred_element_type=F32
    ).astype(out_ref.dtype)


def row_outer(left_array, right_array):
    rows, height = left_array.shape
    width = right_array.shape[1]
    step = 384
    return pl.pallas_call(
        outer_kernel,
        grid=(height // step,),
        in_specs=[
            pl.BlockSpec((rows, step), lambda i: (0, i)),
            pl.BlockSpec((rows, width), lambda i: (0, 0)),
        ],
        out_specs=pl.BlockSpec((step, width), lambda i: (i, 0)),
        out_shape=jax.ShapeDtypeStruct((height, width), BF),
        compiler_params=pltpu.CompilerParams(vmem_limit_bytes=32 * 1024 * 1024),
        cost_estimate=pl.CostEstimate(
            flops=2 * rows * height * width,
            bytes_accessed=2 * (rows * height + rows * width + height * width),
            transcendentals=0,
        ),
        name="row_outer",
    )(left_array, right_array)


def split_kernel(core_ref, left_ref, right_ref, mine_ref, twin_ref, sums_ref):
    chunk = mine_ref.shape[1]
    sums_ref[...] = lax.dot_general(
        left_ref[...], right_ref[...], (((0,), (0,)), ((), ())), preferred_element_type=F32
    )
    for i in range(mine_ref.shape[0]):
        for out_ref, owner in ((mine_ref, core_ref[0]), (twin_ref, 1 - core_ref[0])):
            start = pl.multiple_of((2 * i + owner) * chunk, 8)
            out_ref[i] = sums_ref[pl.ds(start, chunk), :].astype(out_ref.dtype)


def row_outer_split(left_array, right_array, core):
    rows, height = left_array.shape
    width = right_array.shape[1]
    step = 384
    chunk = height // GROUP
    part = jax.ShapeDtypeStruct((CHIPS, chunk, width), BF)
    out_spec = pl.BlockSpec((step // chunk // 2, chunk, width), lambda i, c: (i, 0, 0))
    return pl.pallas_call(
        split_kernel,
        grid_spec=pltpu.PrefetchScalarGridSpec(
            num_scalar_prefetch=1,
            grid=(height // step,),
            in_specs=[
                pl.BlockSpec((rows, step), lambda i, c: (0, i)),
                pl.BlockSpec((rows, width), lambda i, c: (0, 0)),
            ],
            out_specs=[out_spec, out_spec],
            scratch_shapes=[pltpu.VMEM((step, width), F32)],
        ),
        out_shape=[part, part],
        compiler_params=pltpu.CompilerParams(vmem_limit_bytes=32 * 1024 * 1024),
        cost_estimate=pl.CostEstimate(
            flops=2 * rows * height * width,
            bytes_accessed=2 * (rows * height + rows * width + height * width),
            transcendentals=0,
        ),
        name="row_outer_split",
    )(core.reshape(1), left_array, right_array)


def mixer_terms_kernel(
    core_ref, normed_ref, right_ref, mixed_ref, grad_ref, mine_ref, twin_ref, in_ref, out_ref
):
    width = right_ref.shape[1]
    chunk = mine_ref.shape[1]
    half = mixed_ref.shape[1]
    step = in_ref.shape[0]
    owners = ((mine_ref, core_ref[0]), (twin_ref, 1 - core_ref[0]))
    for i in range(normed_ref.shape[1] // step):
        in_ref[...] = lax.dot_general(
            normed_ref[:, i * step : (i + 1) * step],
            right_ref[...],
            (((0,), (0,)), ((), ())),
            preferred_element_type=F32,
        )
        for j in range(step // chunk // 2):
            for part_ref, owner in owners:
                start = pl.multiple_of((2 * j + owner) * chunk, 8)
                part_ref[i * (step // chunk // 2) + j, :, :width] = in_ref[
                    pl.ds(start, chunk), :
                ].astype(BF)
    for i in range(2):
        out_ref[...] = lax.dot_general(
            mixed_ref[...],
            grad_ref[:, i * half : (i + 1) * half],
            (((0,), (0,)), ((), ())),
            preferred_element_type=F32,
        )
        for j in range(CHIPS):
            for part_ref, owner in owners:
                start = pl.multiple_of((2 * j + owner) * (chunk // 2), 8)
                part_ref[j, i * (chunk // 2) : (i + 1) * (chunk // 2), width:] = out_ref[
                    pl.ds(start, chunk // 2), :
                ].astype(BF)


def mixer_terms(normed, rights, mixed, grad_pair, core):
    rows, height = normed.shape
    width = rights.shape[1]
    half = mixed.shape[1]
    part = jax.ShapeDtypeStruct((CHIPS, height // GROUP, width + half), BF)
    whole = pl.BlockSpec(memory_space=pltpu.VMEM)
    return pl.pallas_call(
        mixer_terms_kernel,
        in_specs=[pl.BlockSpec(memory_space=pltpu.SMEM)] + [whole] * 4,
        out_specs=[whole, whole],
        out_shape=[part, part],
        scratch_shapes=[pltpu.VMEM((384, width), F32), pltpu.VMEM((half, half), F32)],
        compiler_params=pltpu.CompilerParams(vmem_limit_bytes=48 * 1024 * 1024),
        cost_estimate=pl.CostEstimate(
            flops=2 * rows * height * (width + half),
            bytes_accessed=2 * height * (width + half),
            transcendentals=0,
        ),
        name="mixer_terms",
    )(core.reshape(1), normed, rights, mixed, grad_pair)


def owned_kernel(side_ref, own_ref, came_ref, *out_refs):
    first = side_ref[0] == 0
    width = own_ref.shape[3]
    for i in range(CHIPS):
        for j, out_ref in enumerate(out_refs):
            own, came = own_ref[i, j].astype(F32), came_ref[i, j].astype(F32)
            out_ref[:, i * width : (i + 1) * width] = jnp.concatenate(
                [jnp.where(first, own, came), jnp.where(first, came, own)], axis=0
            )


def owned_rows(own, came, side):
    depth, width = 2 * own.shape[2], CHIPS * own.shape[3]
    whole = pl.BlockSpec(memory_space=pltpu.VMEM)
    return pl.pallas_call(
        owned_kernel,
        in_specs=[pl.BlockSpec(memory_space=pltpu.SMEM), whole, whole],
        out_specs=[whole] * 3,
        out_shape=[jax.ShapeDtypeStruct((depth, width), F32)] * 3,
        compiler_params=pltpu.CompilerParams(vmem_limit_bytes=48 * 1024 * 1024),
        cost_estimate=pl.CostEstimate(
            flops=0, bytes_accessed=18 * depth * width, transcendentals=0
        ),
        name="owned_rows",
    )(side.reshape(1), own, came)


def prepare(queries, keys_in, head_gain_pair, positions):
    return (
        rotate(norm_rows(queries, head_gain_pair[0]), positions),
        rotate(norm_rows(keys_in, head_gain_pair[1]), positions),
    )


def attention_parts(normed, first_matrix, pair_matrix, head_gain_pair, segments, positions):
    row_count = normed.shape[0]
    kv_heads = KV_HEADS // SIDES
    group_size = HEADS // KV_HEADS
    queries = forward_dot(normed, first_matrix).reshape(row_count, HEADS // SIDES, HEAD_DIM)
    key_values = forward_dot(normed, pair_matrix).reshape(row_count, 2, kv_heads, HEAD_DIM)
    queries_rot, keys_rot = prepare(queries, key_values[:, 0], head_gain_pair, positions)
    queries_low = queries_rot.astype(BF).reshape(row_count, kv_heads, group_size, HEAD_DIM)
    keys_low = keys_rot.astype(BF)
    values_low = key_values[:, 1].astype(BF)
    offsets = jnp.arange(row_count)
    allowed = (segments[:, None] == segments[None, :]) & (offsets[:, None] >= offsets[None, :])
    scale_factor = HEAD_DIM ** (-0.5)
    scores = (
        jnp.einsum("qhgd,khd->hgqk", queries_low, keys_low, preferred_element_type=F32)
        * scale_factor
    )
    scores = jnp.where(allowed, scores, MASKED_SCORE)
    probabilities = jax.nn.softmax(scores, axis=-1)
    probs_low = probabilities.astype(BF)
    mixed = jnp.einsum("hgqk,khd->qhgd", probs_low, values_low, preferred_element_type=F32)
    mixed = mixed.reshape(row_count, -1).astype(BF)
    return (
        mixed,
        (queries, key_values, queries_low, keys_low, values_low, probabilities, probs_low),
    )


def attention_back(grad_out, context, first_matrix, pair_matrix, head_gain_pair, positions):
    queries, key_values, queries_low, keys_low, values_low, probabilities, probs_low = context
    row_count = grad_out.shape[0]
    kv_heads = KV_HEADS // SIDES
    group_size = HEADS // KV_HEADS
    scale_factor = HEAD_DIM ** (-0.5)
    grad_low = grad_out.astype(BF).reshape(row_count, kv_heads, group_size, HEAD_DIM)
    grad_probs = jnp.einsum("qhgd,khd->hgqk", grad_low, values_low, preferred_element_type=F32)
    grad_values = jnp.einsum("hgqk,qhgd->khd", probs_low, grad_low, preferred_element_type=F32)
    grad_scores = probabilities * (
        grad_probs - jnp.sum(grad_probs * probabilities, axis=-1, keepdims=True)
    )
    grad_scores = grad_scores.astype(BF)
    grad_queries = (
        jnp.einsum("hgqk,khd->qhgd", grad_scores, keys_low, preferred_element_type=F32)
        * scale_factor
    )
    grad_keys = (
        jnp.einsum("hgqk,qhgd->khd", grad_scores, queries_low, preferred_element_type=F32)
        * scale_factor
    )

    def prepared(query_in, key_in, gain_in):
        return prepare(query_in, key_in, gain_in, positions)

    unused_value, pull_prep = jax.vjp(prepared, queries, key_values[:, 0], head_gain_pair)
    grad_query_pre, grad_key_pre, grad_head = pull_prep(
        (grad_queries.reshape(queries.shape), grad_keys)
    )
    grad_first = grad_query_pre.reshape(row_count, -1).astype(BF)
    grad_pairs = (
        jnp.stack([grad_key_pre, grad_values], axis=1).reshape(row_count, -1).astype(BF)
    )
    grad_normed = back_dot(grad_first, first_matrix) + back_dot(grad_pairs, pair_matrix)
    return (grad_normed, grad_first, grad_pairs, grad_head)


def conv_mix(signal, gate_pair, kernel_rows, positions):
    width = signal.shape[-1]
    carried = gate_pair[:, :width] * signal
    summed = kernel_rows[0] * carried
    for lag_steps in (1, 2):
        delayed = jnp.concatenate(
            [jnp.zeros((lag_steps, width), F32), carried[:-lag_steps]], axis=0
        )
        summed = summed + kernel_rows[lag_steps] * jnp.where(
            (positions >= lag_steps)[:, None], delayed, 0.0
        )
    return gate_pair[:, width:] * summed


def conv_parts(normed, first_matrix, gating_matrix, kernel_rows, positions):
    signal = forward_dot(normed, first_matrix)
    gate_pair = forward_dot(normed, gating_matrix)
    mixed = conv_mix(signal, gate_pair, kernel_rows, positions).astype(BF)
    return (mixed, (signal, gate_pair))


def conv_back(grad_out, context, first_matrix, gating_matrix, kernel_rows, positions):
    signal, gate_pair = context

    def mixing(signal_in, gates_in, kernel_in):
        return conv_mix(signal_in, gates_in, kernel_in, positions)

    unused_value, pull_conv = jax.vjp(mixing, signal, gate_pair, kernel_rows)
    grad_signal, grad_gates, grad_kernel = pull_conv(grad_out)
    grad_first = grad_signal.astype(BF)
    grad_gates = grad_gates.astype(BF)
    grad_normed = back_dot(grad_first, first_matrix) + back_dot(grad_gates, gating_matrix)
    return (grad_normed, grad_first, grad_gates, grad_kernel)


def glu_unit(gate_in, up_in):
    return jax.nn.silu(gate_in) * up_in


def on_device(
    section_inputs,
    seq_lengths,
    norm_gains,
    head_gains,
    conv_kernel,
    first_weight,
    out_weight,
    gate_weight,
    up_weight,
    down_weight,
    pair_weight,
    gating_weight,
):
    side = lax.axis_index("section")
    on_first = side == 0
    shards = lax.axis_size("fsdp")
    outer = shards // GROUP
    place = lax.axis_index("fsdp")
    core = place % 2
    on_core0 = core == 0
    same_core = [
        [GROUP * o + 2 * a + c for a in range(CHIPS)] for o in range(outer) for c in range(2)
    ]
    across = [[GROUP * o + i for o in range(outer)] for i in range(GROUP)]
    depth = first_weight.shape[1]
    model_width = first_weight.shape[2]
    half_width = model_width // SIDES
    pair_half = pair_weight.shape[1] // 2 // SIDES
    hidden_part = gate_weight.shape[2] // CHIPS

    def pick(first_value, second_value):
        return jnp.where(on_first, first_value, second_value)

    def half_of(columns, width):
        return lax.dynamic_slice_in_dim(columns, side * width, width, axis=1)

    def other_half_of(columns, width):
        return lax.dynamic_slice_in_dim(columns, (1 - side) * width, width, axis=1)

    rows = section_inputs[0]
    arrived = other_side(pick(rows[TOK_MB:], rows[:TOK_MB]))
    start_rows = pick(rows[:TOK_MB], arrived).astype(F32)
    cotangent = pick(arrived, rows[TOK_MB:])
    segments, positions, valid = layout(seq_lengths)
    own_valid = pick(valid[0], valid[1])[:, None]
    segments = segments + 8 * jnp.arange(2, dtype=jnp.int32)[:, None]
    segments = pick(segments.reshape(-1), segments[::-1].reshape(-1))
    positions = pick(positions.reshape(-1), positions[::-1].reshape(-1))

    first_kept = half_of(first_weight[0], half_width)
    first_came = other_side(other_half_of(first_weight[0], half_width))
    pair_own = jnp.concatenate(
        [
            half_of(pair_weight[:, : pair_half * SIDES], pair_half),
            half_of(pair_weight[:, pair_half * SIDES :], pair_half),
        ],
        axis=1,
    )
    gating_own = jnp.concatenate(
        [
            half_of(gating_weight[:, :model_width], half_width),
            half_of(gating_weight[:, model_width:], half_width),
        ],
        axis=1,
    )
    out_kept = out_weight[0].reshape(2, depth // 2, model_width)

    def out_pairs(block, part):
        sides = shards // SIDES
        return [
            (block * shards + j, (j // sides) * shards + 2 * (j % sides) + part)
            for j in range(shards)
        ]

    def out_shard(block):
        parts = [
            lax.ppermute(out_kept[part], ("section", "fsdp"), out_pairs(block, part))
            for part in range(2)
        ]
        return jnp.where(place % 2 == 0, parts[0], parts[1])

    def section_rows(matrix):
        if outer > 1:
            matrix = lax.all_gather(
                matrix, "fsdp", axis=0, tiled=True, axis_index_groups=across
            )
        return matrix

    def row_half(matrix, which):
        return lax.dynamic_slice_in_dim(
            matrix, which * (matrix.shape[0] // 2), matrix.shape[0] // 2, axis=0
        )

    def chunks(matrix):
        return matrix.reshape(-1, CHIPS, hidden_part).transpose(1, 0, 2)

    def exchanged(chunks):
        return lax.all_to_all(chunks, "fsdp", 0, 0, axis_index_groups=same_core)

    def assembled(mine, swapped):
        twin = other_core(mine, outer)
        twin_swapped = other_core(swapped, outer)
        whole = []
        for j in range(3):
            a, b, c, d = (v[:, j] for v in (mine, swapped, twin, twin_swapped))
            lower, lower_swapped = jnp.where(on_core0, a, c), jnp.where(on_core0, b, d)
            upper, upper_swapped = jnp.where(on_core0, c, a), jnp.where(on_core0, d, b)
            both = jnp.stack(
                [
                    jnp.concatenate(
                        [pick(lower, lower_swapped), pick(lower_swapped, lower)], axis=1
                    ),
                    jnp.concatenate(
                        [pick(upper, upper_swapped), pick(upper_swapped, upper)], axis=1
                    ),
                ],
                axis=1,
            )
            both = both.reshape(CHIPS, 2, outer, depth, hidden_part)
            whole.append(both.transpose(2, 0, 1, 3, 4).reshape(model_width, hidden_part))
        return whole

    def out_flat(part):
        return jnp.concatenate([part[:, :half_width], part[:, half_width:]], axis=0)

    def out_matrix(flat):
        flat = flat.reshape(shards, 2, depth // 2, half_width)
        return jnp.concatenate(
            [flat[:, i].reshape(half_width, half_width) for i in range(2)], axis=1
        )

    attention_part = jnp.concatenate(
        [pick(first_kept, first_came), pair_own, out_flat(out_shard(0))], axis=1
    )
    conv_part = jnp.concatenate(
        [pick(first_came, first_kept), gating_own, out_flat(out_shard(1))], axis=1
    )
    attention_all = lax.all_gather(attention_part, "fsdp", axis=0, tiled=True)
    matrices = [section_rows(m) for m in (gate_weight[0], up_weight[0], down_weight[0].T)]
    sent_raw, unused_first = pinned([row_half(m, 1 - side) for m in matrices], first_came)
    came_raw = [other_side(m) for m in sent_raw]
    kept_raw = [row_half(m, side) for m in matrices]
    laid0 = exchanged(
        jnp.stack([chunks(pick(k, c)) for k, c in zip(kept_raw, came_raw)], axis=1)
    )

    first_half0 = attention_all[:, :half_width]
    pair_part = attention_all[:, half_width : half_width + 2 * pair_half]
    out_half0 = out_matrix(attention_all[:, half_width + 2 * pair_half :])
    kernel_half = half_of(conv_kernel, half_width)

    def paired(own):
        return jnp.concatenate([own, other_side(own)], axis=0)

    def pair_sum(terms):
        return terms[:TOK_MB] + other_side(terms[TOK_MB:].astype(BF)).astype(F32)

    def feed_forward(all_h, mlp):
        gate_pre = forward_dot(all_h, mlp[0])
        up_pre = forward_dot(all_h, mlp[1])
        active = glu_unit(gate_pre, up_pre).astype(BF)
        return (back_dot(active, mlp[2]), (all_h, gate_pre, up_pre, active))

    def feed_back(all_up, saved, mlp):
        all_h, gate_pre, up_pre, active = saved
        grad_active = forward_dot(all_up, mlp[2])
        unused_value, pull_glu = jax.vjp(glu_unit, gate_pre, up_pre)
        grad_gate, grad_up = pull_glu(grad_active)
        grad_gate = grad_gate.astype(BF)
        grad_up = grad_up.astype(BF)
        terms = tuple(
            outer_split(left, right)
            for left, right in ((all_h, grad_gate), (all_h, grad_up), (all_up, active))
        )
        return (back_dot(grad_gate, mlp[0]) + back_dot(grad_up, mlp[1]), terms)

    def outer_split(left, right):
        if outer == 1:
            return row_outer_split(left, right, core)
        term = row_outer(left, right).astype(F32)
        term = lax.psum(term, "fsdp", axis_index_groups=across).astype(BF)
        term = term.reshape(outer, CHIPS, 2, depth, hidden_part).transpose(2, 1, 0, 3, 4)
        term = term.reshape(2, CHIPS, outer * depth, hidden_part)
        return tuple(
            lax.dynamic_index_in_dim(term, owner, 0, keepdims=False) for owner in (core, 1 - core)
        )

    def out_blocks(term):
        parts = [
            term[:, i * half_width : (i + 1) * half_width].reshape(shards, -1, half_width)
            for i in range(2)
        ]
        return jnp.concatenate(parts, axis=1).reshape(model_width, half_width)

    def out_unblocks(rows_of):
        return jnp.concatenate([rows_of[: depth // 2], rows_of[depth // 2 :]], axis=1)

    def mixer_cores(normed, rights, mixed, grad_pair):
        rights = jnp.concatenate(rights, axis=1)
        if outer == 1:
            mine, twin = mixer_terms(normed, rights, mixed, grad_pair, core)
            return mine, other_core(twin, outer)
        term = jnp.concatenate(
            [row_outer(normed, rights), out_blocks(row_outer(mixed, grad_pair))], axis=1
        )
        return lax.psum_scatter(term, "fsdp", scatter_dimension=0, tiled=True)

    def mixer_sum(cores):
        return Scattered(cores) if outer > 1 else chip_sum(cores, place, outer)

    normed0 = paired(norm_rows(start_rows, norm_gains[0, 0]).astype(BF))
    mixed0, context0 = attention_parts(
        normed0, first_half0, pair_part, head_gains, segments, positions
    )
    hidden0 = start_rows + pair_sum(forward_dot(mixed0, out_half0))
    hidden0, laid0, conv_part = pinned(hidden0, laid0, conv_part)
    swapped0 = other_side(laid0)
    conv_all = lax.all_gather(conv_part, "fsdp", axis=0, tiled=True)
    normed_h0 = norm_rows(hidden0, norm_gains[0, 1]).astype(BF)
    all_h0 = ring_gather(normed_h0, outer)
    all_h0, swapped0 = pinned(all_h0, swapped0)
    mlp0 = assembled(laid0, swapped0)
    fed_term0, saved0 = feed_forward(all_h0, mlp0)
    fed0 = ring_scatter(fed_term0, outer)[0]
    raw1, fed0 = pinned([pick(c, k) for k, c in zip(kept_raw, came_raw)], fed0)
    laid1 = exchanged(jnp.stack([chunks(m) for m in raw1], axis=1))
    middle = (hidden0 + fed0).astype(BF)

    middle_rows = middle.astype(F32)
    first_half1 = conv_all[:, :half_width]
    gating_part = conv_all[:, half_width : 3 * half_width]
    out_half1 = out_matrix(conv_all[:, 3 * half_width :])
    normed1 = paired(norm_rows(middle_rows, norm_gains[1, 0]).astype(BF))
    mixed1, context1 = conv_parts(normed1, first_half1, gating_part, kernel_half, positions)
    hidden1 = middle_rows + pair_sum(forward_dot(mixed1, out_half1))
    normed_h1 = norm_rows(hidden1, norm_gains[1, 1]).astype(BF)
    nothing = jnp.zeros_like(cotangent)
    upstream1 = jnp.where(own_valid, cotangent, nothing)
    both = ring_blocks(jnp.concatenate([normed_h1, upstream1], axis=0), outer)
    all_h1 = jnp.concatenate([part[:TOK_MB] for part in both], axis=0)
    all_up1 = jnp.concatenate([part[TOK_MB:] for part in both], axis=0)
    all_h1, all_up1, swapped1 = pinned(all_h1, all_up1, other_side(laid1))
    mlp1 = assembled(laid1, swapped1)
    fed_term1, saved1 = feed_forward(all_h1, mlp1)

    def core_sum(terms):
        return [
            (mine.astype(F32) + other_core(twin, outer).astype(F32))
            .astype(BF)
            .reshape(CHIPS, 2, -1, hidden_part)
            for mine, twin in terms
        ]

    def side_sum(terms):
        kept = [lax.dynamic_index_in_dim(t, side, 1, keepdims=False) for t in terms]
        sent = [lax.dynamic_index_in_dim(t, 1 - side, 1, keepdims=False) for t in terms]
        return [
            (k.astype(F32) + other_side(t).astype(F32)).astype(BF) for k, t in zip(kept, sent)
        ]

    back_term1, terms1 = feed_back(all_up1, saved1, mlp1)
    grad_h1, terms1 = ring_scatter(back_term1, outer, terms1)
    unused_norm, pull_hidden1 = jax.vjp(norm_rows, hidden1, norm_gains[1, 1])
    grad_hidden1, gain_h1 = pull_hidden1(grad_h1)
    grad_hidden1 = grad_hidden1 + upstream1.astype(F32)
    grad_pair1 = paired(grad_hidden1.astype(BF))
    cores1 = core_sum(terms1)
    grad_pair1, cores1, fed_term1 = pinned(grad_pair1, cores1, fed_term1)
    final = (hidden1 + ring_scatter(fed_term1, outer)[0]).astype(BF)
    sides1 = side_sum(cores1)
    grad_normed1, grad_first1, grad_gating, grad_kernel = conv_back(
        back_dot(grad_pair1, out_half1), context1, first_half1, gating_part, kernel_half, positions
    )
    grad_normed1 = pair_sum(grad_normed1)
    unused_norm, pull_start1 = jax.vjp(norm_rows, middle_rows, norm_gains[1, 0])
    grad_start1, gain_x1 = pull_start1(grad_normed1)
    grad_middle = (grad_start1 + grad_hidden1).astype(BF)

    all_up0 = ring_gather(grad_middle, outer)
    conv_cores = mixer_cores(normed1, [grad_first1, grad_gating], mixed1, grad_pair1)
    all_up0, conv_cores, sides1, final = pinned(all_up0, conv_cores, sides1, final)
    sent1 = exchanged(jnp.stack(sides1, axis=1))
    back_term0, terms0 = feed_back(all_up0, saved0, mlp0)
    grad_h0, terms0 = ring_scatter(back_term0, outer, terms0)
    grad_h0, conv_cores, sent1 = pinned(grad_h0, conv_cores, sent1)
    conv_sum = mixer_sum(conv_cores)
    cores0 = core_sum(terms0)
    unused_norm, pull_hidden0 = jax.vjp(norm_rows, hidden0, norm_gains[0, 1])
    grad_hidden0, gain_h0 = pull_hidden0(grad_h0)
    grad_hidden0 = grad_hidden0 + grad_middle.astype(F32)
    grad_pair0, cores0 = conv_sum.step(paired(grad_hidden0.astype(BF)), cores0)
    sides0 = side_sum(cores0)
    grad_normed0, grad_first0, grad_pairs, grad_head = attention_back(
        back_dot(grad_pair0, out_half0), context0, first_half0, pair_part, head_gains, positions
    )
    grad_normed0, grad_first0, grad_pairs, grad_head = conv_sum.step(
        grad_normed0, grad_first0, grad_pairs, grad_head
    )
    (grad_normed0,) = conv_sum.step(pair_sum(grad_normed0))
    (sides0,) = conv_sum.step(sides0)
    conv_sums = conv_sum.total().astype(BF)
    unused_norm, pull_start0 = jax.vjp(norm_rows, start_rows, norm_gains[0, 0])
    grad_start0, gain_x0 = pull_start0(grad_normed0)
    grad_start = (grad_start0 + grad_hidden0).astype(BF)
    sent0 = exchanged(jnp.stack(sides0, axis=1))

    attention_cores = mixer_cores(normed0, [grad_first0, grad_pairs], mixed0, grad_pair0)

    def returned(first_rows, second_rows):
        kept = pick(first_rows, second_rows)
        came = other_side(pick(second_rows, first_rows))
        return jnp.concatenate([pick(kept, came), pick(came, kept)], axis=0)

    activation_rows = returned(
        jnp.where(own_valid, middle, nothing), jnp.where(own_valid, final, nothing)
    )
    input_rows = returned(grad_start, grad_middle)

    kernel_whole = lax.dynamic_update_slice_in_dim(
        jnp.zeros_like(conv_kernel), grad_kernel, side * half_width, axis=1
    )
    head_row = jnp.pad(grad_head.reshape(1, -1), ((0, 0), (0, model_width - grad_head.size)))
    small = jnp.concatenate(
        [jnp.stack([gain_x0, gain_h0, gain_x1, gain_h1]), kernel_whole, head_row], axis=0
    )
    sent0, attention_cores, input_rows, activation_rows, small = pinned(
        sent0, attention_cores, input_rows, activation_rows, everywhere(small)
    )
    sent_came = other_side(pick(sent1, sent0))
    def owned(number):
        own = pick(sent0[:, number], sent1[:, number])
        came = sent_came[:, number]
        rows_of = jnp.concatenate([pick(own, came), pick(came, own)], axis=1)
        rows_of = rows_of.transpose(1, 0, 2).reshape(outer, depth, -1)
        return lax.dynamic_index_in_dim(rows_of, place // GROUP, 0, keepdims=False).astype(F32)

    attention_sum = mixer_sum(attention_cores)
    attention_sum.step()
    attention_sum.step()
    (sent_came,) = attention_sum.step(sent_came)
    attention_sums = attention_sum.total().astype(BF)
    if outer == 1:
        grad_gate, grad_up, grad_down = owned_rows(pick(sent0, sent1), sent_came, side)
    else:
        grad_gate, grad_up, grad_down = (owned(number) for number in range(3))
    out_sums0 = out_unblocks(attention_sums[:, half_width + 2 * pair_half :])
    out_sums1 = out_unblocks(conv_sums[:, 3 * half_width :])

    even_place = place % 2 == 0
    out_sent = (
        jnp.where(even_place, out_sums0, out_sums1),
        jnp.where(even_place, out_sums1, out_sums0),
    )
    out_came = [
        lax.ppermute(
            value,
            ("section", "fsdp"),
            [(b, a) for part in range(2) for a, b in out_pairs((part + turn) % 2, part)],
        )
        for turn, value in enumerate(out_sent)
    ]
    out_rows = jnp.concatenate(
        [pick(out_came[0], out_came[1]), pick(out_came[1], out_came[0])], axis=0
    ).astype(F32)

    def both_halves(own_part, came_part):
        return jnp.concatenate([pick(own_part, came_part), pick(came_part, own_part)], axis=1)

    def columns(own, came, width):
        return jnp.concatenate(
            [both_halves(own[:, i : i + width], came[:, i : i + width]) for i in (0, width)], axis=1
        )

    sums = (attention_sums[:, :half_width], conv_sums[:, :half_width])
    pair_own = attention_sums[:, half_width : half_width + 2 * pair_half]
    gating_own = conv_sums[:, half_width : 3 * half_width]
    came = other_side(
        jnp.concatenate([pick(sums[1], sums[0]), pair_own, gating_own], axis=1)
    )
    first_rows = both_halves(pick(sums[0], sums[1]), came[:, :half_width])
    pair_rows = columns(pair_own, came[:, half_width : half_width + 2 * pair_half], pair_half)
    gating_rows = columns(gating_own, came[:, half_width + 2 * pair_half :], half_width)

    return (
        activation_rows[None],
        input_rows[None],
        small[:4].reshape(2, 2, model_width),
        small[7, : grad_head.size].reshape(grad_head.shape),
        small[4:7],
        first_rows.astype(F32)[None],
        out_rows[None],
        grad_gate[None],
        grad_up[None],
        grad_down.T[None],
        pair_rows.astype(F32),
        gating_rows.astype(F32),
    )


def solution(mesh):
    in_specs = (
        P("section", "fsdp", None),
        P("fsdp", None),
        P(),
        P(),
        P(),
        P("section", "fsdp", None),
        P("section", "fsdp", None),
        P("section", "fsdp", None),
        P("section", "fsdp", None),
        P("section", None, "fsdp"),
        P("fsdp", None),
        P("fsdp", None),
    )
    out_specs = (
        P("section", "fsdp", None),
        P("section", "fsdp", None),
        P(),
        P(),
        P(),
        P("section", "fsdp", None),
        P("section", "fsdp", None),
        P("section", "fsdp", None),
        P("section", "fsdp", None),
        P("section", None, "fsdp"),
        P("fsdp", None),
        P("fsdp", None),
    )
    return jax.shard_map(
        on_device, mesh=mesh, in_specs=in_specs, out_specs=out_specs, check_vma=False
    )
```

```python
import jax
import jax.numpy as jnp
from jax import lax
from jax.experimental import pallas as pl
from jax.experimental.pallas import tpu as pltpu
from jax.sharding import PartitionSpec as P

HEADS = 24
KV_HEADS = 8
HEAD_DIM = 64
TOK_MB = 64
SIDES = 2
GROUP = 16
CHIPS = 8
RING = (0, 2, 4, 6, 7, 5, 3, 1)

EPSILON = 1e-05
ROPE_BASE = 1000000.0
MASKED_SCORE = -1000000000.0

BF = jnp.bfloat16
F32 = jnp.float32


def group_pairs(chip_pairs, outer):
    return [
        (GROUP * o + 2 * a + c, GROUP * o + 2 * b + c)
        for o in range(outer)
        for a, b in chip_pairs
        for c in range(2)
    ]


def forward_ring(outer):
    return group_pairs([(RING[i], RING[(i + 1) % CHIPS]) for i in range(CHIPS)], outer)


def backward_ring(outer):
    return group_pairs([(RING[(i + 1) % CHIPS], RING[i]) for i in range(CHIPS)], outer)


def other_core(value, outer):
    return lax.ppermute(value, "fsdp", [(i, i ^ 1) for i in range(GROUP * outer)])


def other_side(value):
    return lax.ppermute(value, "section", [(0, 1), (1, 0)])


def to_side(value, side):
    return lax.ppermute(value, "section", [(1 - side, side)])


ORDER = (0, -1, 1, -2, 2, -3, 3, 4)


def ring_blocks(own, outer):
    fwd, bwd = forward_ring(outer), backward_ring(outer)
    blocks = [own]
    up, down = own, own
    for _ in range(3):
        up, down = lax.ppermute(up, "fsdp", fwd), lax.ppermute(down, "fsdp", bwd)
        blocks += [up, down]
    half = own.shape[1] // 2
    left = lax.ppermute(up[:, :half], "fsdp", fwd)
    right = lax.ppermute(down[:, half:], "fsdp", bwd)
    blocks.append(jnp.concatenate([left, right], axis=1))
    return blocks


def ring_gather(own, outer):
    return jnp.concatenate(ring_blocks(own, outer), axis=0)


class RingSum:
    def __init__(self, blocks, outer):
        self.ways = forward_ring(outer), backward_ring(outer)
        self.block = dict(zip(ORDER, blocks))
        self.half = blocks[0].shape[1] // 2
        self.sums = (self.block[4][:, : self.half], self.block[4][:, self.half :])
        self.left = 3

    def step(self, *values):
        up, down = (
            lax.ppermute(v.astype(BF), "fsdp", way) for v, way in zip(self.sums, self.ways)
        )
        up, down, values = pinned(up, down, values)
        up, down = up.astype(F32), down.astype(F32)
        block, half, left = self.block, self.half, self.left
        if left == 3:
            up = jnp.concatenate([block[3][:, :half] + up, block[3][:, half:]], axis=1)
            down = jnp.concatenate([block[-3][:, :half], block[-3][:, half:] + down], axis=1)
        elif left:
            up, down = block[left] + up, block[-left] + down
        self.sums = (up, down)
        self.left -= 1
        return values

    def total(self):
        while self.left >= 0:
            self.step()
        return self.block[0] + self.sums[0] + self.sums[1]


def row_ring(terms, outer):
    rows = terms.shape[0] // CHIPS
    return RingSum([terms[i * rows : (i + 1) * rows] for i in range(CHIPS)], outer)


def ring_scatter(terms, outer, beside=()):
    ring = row_ring(terms, outer)
    beside = [ring.step(value)[0] for value in beside]
    return ring.total(), beside


def ring_chips(chip):
    odd = chip & 1
    spot = (chip >> 1) * (1 - 2 * odd) + 7 * odd
    spots = [(spot + d) & 7 for d in ORDER]
    return [2 * at + (at >> 2) * (15 - 4 * at) for at in spots]


def chip_sum(terms, place, outer):
    blocks = [
        sum(lax.dynamic_index_in_dim(t, chip, 0, keepdims=False).astype(F32) for t in terms)
        for chip in ring_chips(place // 2)
    ]
    return RingSum(blocks, outer)


class Scattered:
    def __init__(self, rows):
        self.rows = rows

    def step(self, *values):
        return values

    def total(self):
        return self.rows


def everywhere(value):
    value = value + other_side(value)
    for bit in range((lax.axis_size("fsdp") - 1).bit_length()):
        pairs = [(i, i ^ (1 << bit)) for i in range(lax.axis_size("fsdp"))]
        value = value + lax.ppermute(value, "fsdp", pairs)
    return value


def pinned(*values):
    return lax.optimization_barrier(values)


def layout(lengths):
    seq_ends = jnp.cumsum(lengths, axis=-1)
    offsets = jnp.arange(TOK_MB, dtype=jnp.int32)
    passed = (offsets[:, None] >= seq_ends[..., None, :]).astype(jnp.int32)
    segments = jnp.sum(passed, axis=-1)
    positions = offsets - jnp.sum(passed * lengths[..., None, :], axis=-1)
    valid = segments < lengths.shape[-1]
    return (segments, positions, valid)


def norm_rows(values, scale_gain):
    return (
        values * lax.rsqrt(jnp.mean(values * values, axis=-1, keepdims=True) + EPSILON) * scale_gain
    )


def rotate(values, positions):
    half_width = values.shape[-1] // 2
    frequency = ROPE_BASE ** (-2.0 * jnp.arange(half_width, dtype=F32) / values.shape[-1])
    angles = positions.astype(F32)[..., None, None] * frequency
    cosine = jnp.cos(angles)
    sine_part = jnp.sin(angles)
    front_half = values[..., :half_width]
    back_half = values[..., half_width:]
    return jnp.concatenate(
        [front_half * cosine - back_half * sine_part, back_half * cosine + front_half * sine_part],
        axis=-1,
    )


def forward_dot(left_array, right_array):
    return jnp.dot(left_array, right_array, preferred_element_type=F32)


def back_dot(grad_array, weight_array):
    return lax.dot_general(
        grad_array, weight_array, (((1,), (1,)), ((), ())), preferred_element_type=F32
    )


def outer_kernel(left_ref, right_ref, out_ref):
    out_ref[...] = lax.dot_general(
        left_ref[...], right_ref[...], (((0,), (0,)), ((), ())), preferred_element_type=F32
    ).astype(out_ref.dtype)


def row_outer(left_array, right_array):
    rows, height = left_array.shape
    width = right_array.shape[1]
    step = 384
    return pl.pallas_call(
        outer_kernel,
        grid=(height // step,),
        in_specs=[
            pl.BlockSpec((rows, step), lambda i: (0, i)),
            pl.BlockSpec((rows, width), lambda i: (0, 0)),
        ],
        out_specs=pl.BlockSpec((step, width), lambda i: (i, 0)),
        out_shape=jax.ShapeDtypeStruct((height, width), BF),
        compiler_params=pltpu.CompilerParams(vmem_limit_bytes=32 * 1024 * 1024),
        cost_estimate=pl.CostEstimate(
            flops=2 * rows * height * width,
            bytes_accessed=2 * (rows * height + rows * width + height * width),
            transcendentals=0,
        ),
        name="row_outer",
    )(left_array, right_array)


def split_kernel(core_ref, left_ref, right_ref, mine_ref, twin_ref, sums_ref):
    chunk = mine_ref.shape[1]
    sums_ref[...] = lax.dot_general(
        left_ref[...], right_ref[...], (((0,), (0,)), ((), ())), preferred_element_type=F32
    )
    for i in range(mine_ref.shape[0]):
        for out_ref, owner in ((mine_ref, core_ref[0]), (twin_ref, 1 - core_ref[0])):
            start = pl.multiple_of((2 * i + owner) * chunk, 8)
            out_ref[i] = sums_ref[pl.ds(start, chunk), :].astype(out_ref.dtype)


def row_outer_split(left_array, right_array, core):
    rows, height = left_array.shape
    width = right_array.shape[1]
    step = 384
    chunk = height // GROUP
    part = jax.ShapeDtypeStruct((CHIPS, chunk, width), BF)
    out_spec = pl.BlockSpec((step // chunk // 2, chunk, width), lambda i, c: (i, 0, 0))
    return pl.pallas_call(
        split_kernel,
        grid_spec=pltpu.PrefetchScalarGridSpec(
            num_scalar_prefetch=1,
            grid=(height // step,),
            in_specs=[
                pl.BlockSpec((rows, step), lambda i, c: (0, i)),
                pl.BlockSpec((rows, width), lambda i, c: (0, 0)),
            ],
            out_specs=[out_spec, out_spec],
            scratch_shapes=[pltpu.VMEM((step, width), F32)],
        ),
        out_shape=[part, part],
        compiler_params=pltpu.CompilerParams(vmem_limit_bytes=32 * 1024 * 1024),
        cost_estimate=pl.CostEstimate(
            flops=2 * rows * height * width,
            bytes_accessed=2 * (rows * height + rows * width + height * width),
            transcendentals=0,
        ),
        name="row_outer_split",
    )(core.reshape(1), left_array, right_array)


def mixer_terms_kernel(
    core_ref, normed_ref, right_ref, mixed_ref, grad_ref, mine_ref, twin_ref, in_ref, out_ref
):
    width = right_ref.shape[1]
    chunk = mine_ref.shape[1]
    half = mixed_ref.shape[1]
    step = in_ref.shape[0]
    owners = ((mine_ref, core_ref[0]), (twin_ref, 1 - core_ref[0]))
    for i in range(normed_ref.shape[1] // step):
        in_ref[...] = lax.dot_general(
            normed_ref[:, i * step : (i + 1) * step],
            right_ref[...],
            (((0,), (0,)), ((), ())),
            preferred_element_type=F32,
        )
        for j in range(step // chunk // 2):
            for part_ref, owner in owners:
                start = pl.multiple_of((2 * j + owner) * chunk, 8)
                part_ref[i * (step // chunk // 2) + j, :, :width] = in_ref[
                    pl.ds(start, chunk), :
                ].astype(BF)
    for i in range(2):
        out_ref[...] = lax.dot_general(
            mixed_ref[...],
            grad_ref[:, i * half : (i + 1) * half],
            (((0,), (0,)), ((), ())),
            preferred_element_type=F32,
        )
        for j in range(CHIPS):
            for part_ref, owner in owners:
                start = pl.multiple_of((2 * j + owner) * (chunk // 2), 8)
                part_ref[j, i * (chunk // 2) : (i + 1) * (chunk // 2), width:] = out_ref[
                    pl.ds(start, chunk // 2), :
                ].astype(BF)


def mixer_terms(normed, rights, mixed, grad_pair, core):
    rows, height = normed.shape
    width = rights.shape[1]
    half = mixed.shape[1]
    part = jax.ShapeDtypeStruct((CHIPS, height // GROUP, width + half), BF)
    whole = pl.BlockSpec(memory_space=pltpu.VMEM)
    return pl.pallas_call(
        mixer_terms_kernel,
        in_specs=[pl.BlockSpec(memory_space=pltpu.SMEM)] + [whole] * 4,
        out_specs=[whole, whole],
        out_shape=[part, part],
        scratch_shapes=[pltpu.VMEM((384, width), F32), pltpu.VMEM((half, half), F32)],
        compiler_params=pltpu.CompilerParams(vmem_limit_bytes=48 * 1024 * 1024),
        cost_estimate=pl.CostEstimate(
            flops=2 * rows * height * (width + half),
            bytes_accessed=2 * height * (width + half),
            transcendentals=0,
        ),
        name="mixer_terms",
    )(core.reshape(1), normed, rights, mixed, grad_pair)


def owned_kernel(side_ref, *refs):
    own0_ref, *came0_refs = refs[:3]
    own1_ref, *came1_refs = refs[3:6]
    width = own0_ref.shape[3]
    half = came0_refs[0].shape[0]

    def write(own_ref, came_refs, own_first):
        for i in range(CHIPS):
            for j, out_ref in enumerate(refs[6:]):
                rows = [own_ref[i, j].astype(F32), came_refs[i // half][i % half, j].astype(F32)]
                out_ref[:, i * width : (i + 1) * width] = jnp.concatenate(
                    rows if own_first else rows[::-1], axis=0
                )

    pl.when(side_ref[0] == 0)(lambda: write(own0_ref, came0_refs, True))
    pl.when(side_ref[0] == 1)(lambda: write(own1_ref, came1_refs, False))


def owned_rows(own0, came0, own1, came1, side):
    depth, width = 2 * own0.shape[2], CHIPS * own0.shape[3]
    whole = pl.BlockSpec(memory_space=pltpu.VMEM)
    return pl.pallas_call(
        owned_kernel,
        in_specs=[pl.BlockSpec(memory_space=pltpu.SMEM)] + [whole] * 6,
        out_specs=[whole] * 3,
        out_shape=[jax.ShapeDtypeStruct((depth, width), F32)] * 3,
        compiler_params=pltpu.CompilerParams(vmem_limit_bytes=48 * 1024 * 1024),
        cost_estimate=pl.CostEstimate(
            flops=0, bytes_accessed=24 * depth * width, transcendentals=0
        ),
        name="owned_rows",
    )(side.reshape(1), own0, *came0, own1, *came1)


def prepare(queries, keys_in, head_gain_pair, positions):
    return (
        rotate(norm_rows(queries, head_gain_pair[0]), positions),
        rotate(norm_rows(keys_in, head_gain_pair[1]), positions),
    )


def attention_parts(normed, first_matrix, pair_matrix, head_gain_pair, segments, positions):
    row_count = normed.shape[0]
    kv_heads = KV_HEADS // SIDES
    group_size = HEADS // KV_HEADS
    queries = forward_dot(normed, first_matrix).reshape(row_count, HEADS // SIDES, HEAD_DIM)
    key_values = forward_dot(normed, pair_matrix).reshape(row_count, 2, kv_heads, HEAD_DIM)
    queries_rot, keys_rot = prepare(queries, key_values[:, 0], head_gain_pair, positions)
    queries_low = queries_rot.astype(BF).reshape(row_count, kv_heads, group_size, HEAD_DIM)
    keys_low = keys_rot.astype(BF)
    values_low = key_values[:, 1].astype(BF)
    offsets = jnp.arange(row_count)
    allowed = (segments[:, None] == segments[None, :]) & (offsets[:, None] >= offsets[None, :])
    scale_factor = HEAD_DIM ** (-0.5)
    scores = (
        jnp.einsum("qhgd,khd->hgqk", queries_low, keys_low, preferred_element_type=F32)
        * scale_factor
    )
    scores = jnp.where(allowed, scores, MASKED_SCORE)
    probabilities = jax.nn.softmax(scores, axis=-1)
    probs_low = probabilities.astype(BF)
    mixed = jnp.einsum("hgqk,khd->qhgd", probs_low, values_low, preferred_element_type=F32)
    mixed = mixed.reshape(row_count, -1).astype(BF)
    return (
        mixed,
        (queries, key_values, queries_low, keys_low, values_low, probabilities, probs_low),
    )


def attention_back(grad_out, context, first_matrix, pair_matrix, head_gain_pair, positions):
    queries, key_values, queries_low, keys_low, values_low, probabilities, probs_low = context
    row_count = grad_out.shape[0]
    kv_heads = KV_HEADS // SIDES
    group_size = HEADS // KV_HEADS
    scale_factor = HEAD_DIM ** (-0.5)
    grad_low = grad_out.astype(BF).reshape(row_count, kv_heads, group_size, HEAD_DIM)
    grad_probs = jnp.einsum("qhgd,khd->hgqk", grad_low, values_low, preferred_element_type=F32)
    grad_values = jnp.einsum("hgqk,qhgd->khd", probs_low, grad_low, preferred_element_type=F32)
    grad_scores = probabilities * (
        grad_probs - jnp.sum(grad_probs * probabilities, axis=-1, keepdims=True)
    )
    grad_scores = grad_scores.astype(BF)
    grad_queries = (
        jnp.einsum("hgqk,khd->qhgd", grad_scores, keys_low, preferred_element_type=F32)
        * scale_factor
    )
    grad_keys = (
        jnp.einsum("hgqk,qhgd->khd", grad_scores, queries_low, preferred_element_type=F32)
        * scale_factor
    )

    def prepared(query_in, key_in, gain_in):
        return prepare(query_in, key_in, gain_in, positions)

    unused_value, pull_prep = jax.vjp(prepared, queries, key_values[:, 0], head_gain_pair)
    grad_query_pre, grad_key_pre, grad_head = pull_prep(
        (grad_queries.reshape(queries.shape), grad_keys)
    )
    grad_first = grad_query_pre.reshape(row_count, -1).astype(BF)
    grad_pairs = (
        jnp.stack([grad_key_pre, grad_values], axis=1).reshape(row_count, -1).astype(BF)
    )
    grad_normed = back_dot(grad_first, first_matrix) + back_dot(grad_pairs, pair_matrix)
    return (grad_normed, grad_first, grad_pairs, grad_head)


def conv_mix(signal, gate_pair, kernel_rows, positions):
    width = signal.shape[-1]
    carried = gate_pair[:, :width] * signal
    summed = kernel_rows[0] * carried
    for lag_steps in (1, 2):
        delayed = jnp.concatenate(
            [jnp.zeros((lag_steps, width), F32), carried[:-lag_steps]], axis=0
        )
        summed = summed + kernel_rows[lag_steps] * jnp.where(
            (positions >= lag_steps)[:, None], delayed, 0.0
        )
    return gate_pair[:, width:] * summed


def conv_parts(normed, first_matrix, gating_matrix, kernel_rows, positions):
    signal = forward_dot(normed, first_matrix)
    gate_pair = forward_dot(normed, gating_matrix)
    mixed = conv_mix(signal, gate_pair, kernel_rows, positions).astype(BF)
    return (mixed, (signal, gate_pair))


def conv_back(grad_out, context, first_matrix, gating_matrix, kernel_rows, positions):
    signal, gate_pair = context

    def mixing(signal_in, gates_in, kernel_in):
        return conv_mix(signal_in, gates_in, kernel_in, positions)

    unused_value, pull_conv = jax.vjp(mixing, signal, gate_pair, kernel_rows)
    grad_signal, grad_gates, grad_kernel = pull_conv(grad_out)
    grad_first = grad_signal.astype(BF)
    grad_gates = grad_gates.astype(BF)
    grad_normed = back_dot(grad_first, first_matrix) + back_dot(grad_gates, gating_matrix)
    return (grad_normed, grad_first, grad_gates, grad_kernel)


def glu_unit(gate_in, up_in):
    return jax.nn.silu(gate_in) * up_in


def on_device(
    section_inputs,
    seq_lengths,
    norm_gains,
    head_gains,
    conv_kernel,
    first_weight,
    out_weight,
    gate_weight,
    up_weight,
    down_weight,
    pair_weight,
    gating_weight,
):
    side = lax.axis_index("section")
    on_first = side == 0
    shards = lax.axis_size("fsdp")
    outer = shards // GROUP
    place = lax.axis_index("fsdp")
    core = place % 2
    on_core0 = core == 0
    same_core = [
        [GROUP * o + 2 * a + c for a in range(CHIPS)] for o in range(outer) for c in range(2)
    ]
    across = [[GROUP * o + i for o in range(outer)] for i in range(GROUP)]
    depth = first_weight.shape[1]
    model_width = first_weight.shape[2]
    half_width = model_width // SIDES
    pair_half = pair_weight.shape[1] // 2 // SIDES
    hidden_part = gate_weight.shape[2] // CHIPS

    def pick(first_value, second_value):
        return jnp.where(on_first, first_value, second_value)

    def half_of(columns, width):
        return lax.dynamic_slice_in_dim(columns, side * width, width, axis=1)

    def other_half_of(columns, width):
        return lax.dynamic_slice_in_dim(columns, (1 - side) * width, width, axis=1)

    rows = section_inputs[0]
    arrived = other_side(pick(rows[TOK_MB:], rows[:TOK_MB]))
    start_rows = pick(rows[:TOK_MB], arrived).astype(F32)
    cotangent = pick(arrived, rows[TOK_MB:])
    segments, positions, valid = layout(seq_lengths)
    own_valid = pick(valid[0], valid[1])[:, None]
    segments = segments + 8 * jnp.arange(2, dtype=jnp.int32)[:, None]
    segments = pick(segments.reshape(-1), segments[::-1].reshape(-1))
    positions = pick(positions.reshape(-1), positions[::-1].reshape(-1))

    first_kept = half_of(first_weight[0], half_width)
    first_came = other_side(other_half_of(first_weight[0], half_width))
    pair_own = jnp.concatenate(
        [
            half_of(pair_weight[:, : pair_half * SIDES], pair_half),
            half_of(pair_weight[:, pair_half * SIDES :], pair_half),
        ],
        axis=1,
    )
    gating_own = jnp.concatenate(
        [
            half_of(gating_weight[:, :model_width], half_width),
            half_of(gating_weight[:, model_width:], half_width),
        ],
        axis=1,
    )
    out_kept = out_weight[0].reshape(2, depth // 2, model_width)

    def out_pairs(block, part):
        sides = shards // SIDES
        return [
            (block * shards + j, (j // sides) * shards + 2 * (j % sides) + part)
            for j in range(shards)
        ]

    def out_shard(block):
        parts = [
            lax.ppermute(out_kept[part], ("section", "fsdp"), out_pairs(block, part))
            for part in range(2)
        ]
        return jnp.where(place % 2 == 0, parts[0], parts[1])

    def section_rows(matrix):
        if outer > 1:
            matrix = lax.all_gather(
                matrix, "fsdp", axis=0, tiled=True, axis_index_groups=across
            )
        return matrix

    def row_half(matrix, which):
        return lax.dynamic_slice_in_dim(
            matrix, which * (matrix.shape[0] // 2), matrix.shape[0] // 2, axis=0
        )

    def chunks(matrix):
        return matrix.reshape(-1, CHIPS, hidden_part).transpose(1, 0, 2)

    def exchanged(chunks):
        return lax.all_to_all(chunks, "fsdp", 0, 0, axis_index_groups=same_core)

    def assembled(mine, swapped):
        twin = other_core(mine, outer)
        twin_swapped = other_core(swapped, outer)
        whole = []
        for j in range(3):
            a, b, c, d = (v[:, j] for v in (mine, swapped, twin, twin_swapped))
            lower, lower_swapped = jnp.where(on_core0, a, c), jnp.where(on_core0, b, d)
            upper, upper_swapped = jnp.where(on_core0, c, a), jnp.where(on_core0, d, b)
            both = jnp.stack(
                [
                    jnp.concatenate(
                        [pick(lower, lower_swapped), pick(lower_swapped, lower)], axis=1
                    ),
                    jnp.concatenate(
                        [pick(upper, upper_swapped), pick(upper_swapped, upper)], axis=1
                    ),
                ],
                axis=1,
            )
            both = both.reshape(CHIPS, 2, outer, depth, hidden_part)
            whole.append(both.transpose(2, 0, 1, 3, 4).reshape(model_width, hidden_part))
        return whole

    def out_flat(part):
        return jnp.concatenate([part[:, :half_width], part[:, half_width:]], axis=0)

    def out_matrix(flat):
        flat = flat.reshape(shards, 2, depth // 2, half_width)
        return jnp.concatenate(
            [flat[:, i].reshape(half_width, half_width) for i in range(2)], axis=1
        )

    attention_part = jnp.concatenate(
        [pick(first_kept, first_came), pair_own, out_flat(out_shard(0))], axis=1
    )
    conv_part = jnp.concatenate(
        [pick(first_came, first_kept), gating_own, out_flat(out_shard(1))], axis=1
    )
    attention_all = lax.all_gather(attention_part, "fsdp", axis=0, tiled=True)
    matrices = [section_rows(m) for m in (gate_weight[0], up_weight[0], down_weight[0].T)]
    sent_raw, unused_first = pinned([row_half(m, 1 - side) for m in matrices], first_came)
    came_raw = [other_side(m) for m in sent_raw]
    kept_raw = [row_half(m, side) for m in matrices]
    laid0 = exchanged(
        jnp.stack([chunks(pick(k, c)) for k, c in zip(kept_raw, came_raw)], axis=1)
    )

    first_half0 = attention_all[:, :half_width]
    pair_part = attention_all[:, half_width : half_width + 2 * pair_half]
    out_half0 = out_matrix(attention_all[:, half_width + 2 * pair_half :])
    kernel_half = half_of(conv_kernel, half_width)

    def paired(own):
        return jnp.concatenate([own, other_side(own)], axis=0)

    def pair_sum(terms):
        return terms[:TOK_MB] + other_side(terms[TOK_MB:].astype(BF)).astype(F32)

    def feed_forward(all_h, mlp):
        gate_pre = forward_dot(all_h, mlp[0])
        up_pre = forward_dot(all_h, mlp[1])
        active = glu_unit(gate_pre, up_pre).astype(BF)
        return (back_dot(active, mlp[2]), (all_h, gate_pre, up_pre, active))

    def feed_back(all_up, saved, mlp):
        all_h, gate_pre, up_pre, active = saved
        grad_active = forward_dot(all_up, mlp[2])
        unused_value, pull_glu = jax.vjp(glu_unit, gate_pre, up_pre)
        grad_gate, grad_up = pull_glu(grad_active)
        grad_gate = grad_gate.astype(BF)
        grad_up = grad_up.astype(BF)
        terms = tuple(
            outer_split(left, right)
            for left, right in ((all_h, grad_gate), (all_h, grad_up), (all_up, active))
        )
        return (back_dot(grad_gate, mlp[0]) + back_dot(grad_up, mlp[1]), terms)

    def outer_split(left, right):
        if outer == 1:
            return row_outer_split(left, right, core)
        term = row_outer(left, right).astype(F32)
        term = lax.psum(term, "fsdp", axis_index_groups=across).astype(BF)
        term = term.reshape(outer, CHIPS, 2, depth, hidden_part).transpose(2, 1, 0, 3, 4)
        term = term.reshape(2, CHIPS, outer * depth, hidden_part)
        return tuple(
            lax.dynamic_index_in_dim(term, owner, 0, keepdims=False) for owner in (core, 1 - core)
        )

    def out_blocks(term):
        parts = [
            term[:, i * half_width : (i + 1) * half_width].reshape(shards, -1, half_width)
            for i in range(2)
        ]
        return jnp.concatenate(parts, axis=1).reshape(model_width, half_width)

    def out_unblocks(rows_of):
        return jnp.concatenate([rows_of[: depth // 2], rows_of[depth // 2 :]], axis=1)

    def mixer_cores(normed, rights, mixed, grad_pair):
        rights = jnp.concatenate(rights, axis=1)
        if outer == 1:
            mine, twin = mixer_terms(normed, rights, mixed, grad_pair, core)
            return mine, other_core(twin, outer)
        term = jnp.concatenate(
            [row_outer(normed, rights), out_blocks(row_outer(mixed, grad_pair))], axis=1
        )
        return lax.psum_scatter(term, "fsdp", scatter_dimension=0, tiled=True)

    def mixer_sum(cores):
        return Scattered(cores) if outer > 1 else chip_sum(cores, place, outer)

    normed0 = paired(norm_rows(start_rows, norm_gains[0, 0]).astype(BF))
    mixed0, context0 = attention_parts(
        normed0, first_half0, pair_part, head_gains, segments, positions
    )
    hidden0 = start_rows + pair_sum(forward_dot(mixed0, out_half0))
    hidden0, laid0, conv_part = pinned(hidden0, laid0, conv_part)
    swapped0 = other_side(laid0)
    conv_all = lax.all_gather(conv_part, "fsdp", axis=0, tiled=True)
    normed_h0 = norm_rows(hidden0, norm_gains[0, 1]).astype(BF)
    all_h0 = ring_gather(normed_h0, outer)
    all_h0, swapped0 = pinned(all_h0, swapped0)
    mlp0 = assembled(laid0, swapped0)
    fed_term0, saved0 = feed_forward(all_h0, mlp0)
    fed0 = row_ring(fed_term0, outer)
    fed0.step()
    fed0.step()
    (raw1,) = fed0.step([pick(c, k) for k, c in zip(kept_raw, came_raw)])
    fed0 = fed0.total()
    laid1 = exchanged(jnp.stack([chunks(m) for m in raw1], axis=1))
    middle = (hidden0 + fed0).astype(BF)

    middle_rows = middle.astype(F32)
    first_half1 = conv_all[:, :half_width]
    gating_part = conv_all[:, half_width : 3 * half_width]
    out_half1 = out_matrix(conv_all[:, 3 * half_width :])
    normed1 = paired(norm_rows(middle_rows, norm_gains[1, 0]).astype(BF))
    mixed1, context1 = conv_parts(normed1, first_half1, gating_part, kernel_half, positions)
    hidden1 = middle_rows + pair_sum(forward_dot(mixed1, out_half1))
    normed_h1 = norm_rows(hidden1, norm_gains[1, 1]).astype(BF)
    nothing = jnp.zeros_like(cotangent)
    upstream1 = jnp.where(own_valid, cotangent, nothing)
    both = ring_blocks(jnp.concatenate([normed_h1, upstream1], axis=0), outer)
    all_h1 = jnp.concatenate([part[:TOK_MB] for part in both], axis=0)
    all_up1 = jnp.concatenate([part[TOK_MB:] for part in both], axis=0)
    all_h1, all_up1, swapped1 = pinned(all_h1, all_up1, other_side(laid1))
    mlp1 = assembled(laid1, swapped1)
    fed_term1, saved1 = feed_forward(all_h1, mlp1)

    def core_sum(terms):
        return [
            (mine.astype(F32) + other_core(twin, outer).astype(F32))
            .astype(BF)
            .reshape(CHIPS, 2, -1, hidden_part)
            for mine, twin in terms
        ]

    def side_sum(terms):
        kept, sent = (
            jnp.stack(
                [lax.dynamic_index_in_dim(t, which, 1, keepdims=False) for t in terms], axis=1
            )
            for which in (side, 1 - side)
        )
        return (kept.astype(F32) + other_side(sent).astype(F32)).astype(BF)

    back_term1, terms1 = feed_back(all_up1, saved1, mlp1)
    grad_h1, terms1 = ring_scatter(back_term1, outer, terms1)
    unused_norm, pull_hidden1 = jax.vjp(norm_rows, hidden1, norm_gains[1, 1])
    grad_hidden1, gain_h1 = pull_hidden1(grad_h1)
    grad_hidden1 = grad_hidden1 + upstream1.astype(F32)
    grad_hidden1, fed_term1 = pinned(grad_hidden1, fed_term1)
    fed1 = row_ring(fed_term1, outer)
    grad_pair1, cores1 = fed1.step(paired(grad_hidden1.astype(BF)), core_sum(terms1))
    grad_normed1, grad_first1, grad_gating, grad_kernel = conv_back(
        back_dot(grad_pair1, out_half1), context1, first_half1, gating_part, kernel_half, positions
    )
    grad_normed1, grad_first1, grad_gating, grad_kernel = fed1.step(
        grad_normed1, grad_first1, grad_gating, grad_kernel
    )
    (grad_normed1,) = fed1.step(pair_sum(grad_normed1))
    grad_normed1, cores1 = pinned(grad_normed1, cores1)
    sides1 = side_sum(cores1)
    unused_norm, pull_start1 = jax.vjp(norm_rows, middle_rows, norm_gains[1, 0])
    grad_start1, gain_x1 = pull_start1(grad_normed1)
    grad_middle = (grad_start1 + grad_hidden1).astype(BF)

    all_up0 = ring_gather(grad_middle, outer)
    conv_cores = mixer_cores(normed1, [grad_first1, grad_gating], mixed1, grad_pair1)
    final = (hidden1 + fed1.total()).astype(BF)
    all_up0, conv_cores, final = pinned(all_up0, conv_cores, final)
    back_term0, terms0 = feed_back(all_up0, saved0, mlp0)
    ring = row_ring(back_term0, outer)
    terms0 = [ring.step(term)[0] for term in terms0[:2]] + [terms0[2]]
    terms0[2], sides1 = ring.step(terms0[2], sides1)
    grad_h0 = ring.total()
    grad_h0, conv_cores = pinned(grad_h0, conv_cores)
    conv_sum = mixer_sum(conv_cores)
    cores0 = core_sum(terms0)
    unused_norm, pull_hidden0 = jax.vjp(norm_rows, hidden0, norm_gains[0, 1])
    grad_hidden0, gain_h0 = pull_hidden0(grad_h0)
    grad_hidden0 = grad_hidden0 + grad_middle.astype(F32)
    grad_pair0, cores0 = conv_sum.step(paired(grad_hidden0.astype(BF)), cores0)
    grad_normed0, grad_first0, grad_pairs, grad_head = attention_back(
        back_dot(grad_pair0, out_half0), context0, first_half0, pair_part, head_gains, positions
    )
    grad_normed0, grad_first0, grad_pairs, grad_head = conv_sum.step(
        grad_normed0, grad_first0, grad_pairs, grad_head
    )
    (grad_normed0,) = conv_sum.step(pair_sum(grad_normed0))
    grad_normed0, cores0 = pinned(grad_normed0, cores0)
    sides0 = side_sum(cores0)
    conv_sums = conv_sum.total().astype(BF)
    conv_sums, sides1 = pinned(conv_sums, sides1)
    sent1 = exchanged(sides1)
    unused_norm, pull_start0 = jax.vjp(norm_rows, start_rows, norm_gains[0, 0])
    grad_start0, gain_x0 = pull_start0(grad_normed0)
    grad_start = (grad_start0 + grad_hidden0).astype(BF)
    sides0, sent1 = pinned(sides0, sent1)
    sent0 = exchanged(sides0)

    attention_cores = mixer_cores(normed0, [grad_first0, grad_pairs], mixed0, grad_pair0)

    def returned(first_rows, second_rows):
        kept = pick(first_rows, second_rows)
        came = other_side(pick(second_rows, first_rows))
        return jnp.concatenate([pick(kept, came), pick(came, kept)], axis=0)

    activation_rows = returned(
        jnp.where(own_valid, middle, nothing), jnp.where(own_valid, final, nothing)
    )
    input_rows = returned(grad_start, grad_middle)

    kernel_whole = lax.dynamic_update_slice_in_dim(
        jnp.zeros_like(conv_kernel), grad_kernel, side * half_width, axis=1
    )
    head_row = jnp.pad(grad_head.reshape(1, -1), ((0, 0), (0, model_width - grad_head.size)))
    small = jnp.concatenate(
        [jnp.stack([gain_x0, gain_h0, gain_x1, gain_h1]), kernel_whole, head_row], axis=0
    )
    conv_came = other_side(conv_sums[:, : 3 * half_width])
    sent0, attention_cores, input_rows, activation_rows, small, conv_came = pinned(
        sent0, attention_cores, input_rows, activation_rows, everywhere(small), conv_came
    )
    half = CHIPS // 2
    came0 = [to_side(part, 0) for part in (sent0[:half], sent0[half:])]
    came1 = [to_side(part, 1) for part in (sent1[:half], sent1[half:])]
    def owned(number):
        own = pick(sent0[:, number], sent1[:, number])
        came = pick(*(jnp.concatenate(c, axis=0)[:, number] for c in (came0, came1)))
        rows_of = jnp.concatenate([pick(own, came), pick(came, own)], axis=1)
        rows_of = rows_of.transpose(1, 0, 2).reshape(outer, depth, -1)
        return lax.dynamic_index_in_dim(rows_of, place // GROUP, 0, keepdims=False).astype(F32)

    attention_sum = mixer_sum(attention_cores)
    attention_sum.step()
    attention_sum.step()
    came0[0], came1[0] = attention_sum.step(came0[0], came1[0])
    attention_sums = attention_sum.total().astype(BF)
    attention_came = other_side(attention_sums[:, : half_width + 2 * pair_half])
    out_sums0 = out_unblocks(attention_sums[:, half_width + 2 * pair_half :])
    out_sums1 = out_unblocks(conv_sums[:, 3 * half_width :])

    even_place = place % 2 == 0
    out_sent = (
        jnp.where(even_place, out_sums0, out_sums1),
        jnp.where(even_place, out_sums1, out_sums0),
    )
    out_came = [
        lax.ppermute(
            value,
            ("section", "fsdp"),
            [(b, a) for part in range(2) for a, b in out_pairs((part + turn) % 2, part)],
        )
        for turn, value in enumerate(out_sent)
    ]
    out_rows = jnp.concatenate(
        [pick(out_came[0], out_came[1]), pick(out_came[1], out_came[0])], axis=0
    ).astype(F32)

    def both_halves(own_part, came_part):
        return jnp.concatenate([pick(own_part, came_part), pick(came_part, own_part)], axis=1)

    def columns(own, came, width, start):
        return jnp.concatenate(
            [
                both_halves(own[:, i : i + width], came[:, i : i + width])
                for i in (start, start + width)
            ],
            axis=1,
        )

    came0, came1, attention_came = pinned(came0, came1, attention_came)
    first_rows = both_halves(
        pick(attention_sums[:, :half_width], conv_sums[:, :half_width]),
        pick(attention_came[:, :half_width], conv_came[:, :half_width]),
    )
    pair_rows = columns(attention_sums, attention_came, pair_half, half_width)
    gating_rows = columns(conv_sums, conv_came, half_width, half_width)

    if outer == 1:
        grad_gate, grad_up, grad_down = owned_rows(sent0, came0, sent1, came1, side)
    else:
        grad_gate, grad_up, grad_down = (owned(number) for number in range(3))

    return (
        activation_rows[None],
        input_rows[None],
        small[:4].reshape(2, 2, model_width),
        small[7, : grad_head.size].reshape(grad_head.shape),
        small[4:7],
        first_rows.astype(F32)[None],
        out_rows[None],
        grad_gate[None],
        grad_up[None],
        grad_down.T[None],
        pair_rows.astype(F32),
        gating_rows.astype(F32),
    )


def solution(mesh):
    in_specs = (
        P("section", "fsdp", None),
        P("fsdp", None),
        P(),
        P(),
        P(),
        P("section", "fsdp", None),
        P("section", "fsdp", None),
        P("section", "fsdp", None),
        P("section", "fsdp", None),
        P("section", None, "fsdp"),
        P("fsdp", None),
        P("fsdp", None),
    )
    out_specs = (
        P("section", "fsdp", None),
        P("section", "fsdp", None),
        P(),
        P(),
        P(),
        P("section", "fsdp", None),
        P("section", "fsdp", None),
        P("section", "fsdp", None),
        P("section", "fsdp", None),
        P("section", None, "fsdp"),
        P("fsdp", None),
        P("fsdp", None),
    )
    return jax.shard_map(
        on_device, mesh=mesh, in_specs=in_specs, out_specs=out_specs, check_vma=False
    )
```

```python
import jax
import jax.numpy as jnp
from jax import lax
from jax.experimental import pallas as pl
from jax.experimental.pallas import tpu as pltpu
from jax.sharding import PartitionSpec as P

HEADS = 24
KV_HEADS = 8
HEAD_DIM = 64
TOK_MB = 64
SIDES = 2
GROUP = 16
CHIPS = 8
RING = (0, 2, 4, 6, 7, 5, 3, 1)

EPSILON = 1e-05
ROPE_BASE = 1000000.0
MASKED_SCORE = -1000000000.0

BF = jnp.bfloat16
F32 = jnp.float32


def group_pairs(chip_pairs, outer):
    return [
        (GROUP * o + 2 * a + c, GROUP * o + 2 * b + c)
        for o in range(outer)
        for a, b in chip_pairs
        for c in range(2)
    ]


def forward_ring(outer):
    return group_pairs([(RING[i], RING[(i + 1) % CHIPS]) for i in range(CHIPS)], outer)


def backward_ring(outer):
    return group_pairs([(RING[(i + 1) % CHIPS], RING[i]) for i in range(CHIPS)], outer)


def other_core(value, outer):
    return lax.ppermute(value, "fsdp", [(i, i ^ 1) for i in range(GROUP * outer)])


def other_side(value):
    return lax.ppermute(value, "section", [(0, 1), (1, 0)])


def to_side(value, side):
    return lax.ppermute(value, "section", [(1 - side, side)])


ORDER = (0, -1, 1, -2, 2, -3, 3, 4)


def ring_blocks(own, outer):
    fwd, bwd = forward_ring(outer), backward_ring(outer)
    blocks = [own]
    up, down = own, own
    for _ in range(3):
        up, down = lax.ppermute(up, "fsdp", fwd), lax.ppermute(down, "fsdp", bwd)
        blocks += [up, down]
    half = own.shape[1] // 2
    left = lax.ppermute(up[:, :half], "fsdp", fwd)
    right = lax.ppermute(down[:, half:], "fsdp", bwd)
    blocks.append(jnp.concatenate([left, right], axis=1))
    return blocks


def ring_gather(own, outer):
    return jnp.concatenate(ring_blocks(own, outer), axis=0)


class RingSum:
    def __init__(self, blocks, outer):
        self.ways = forward_ring(outer), backward_ring(outer)
        self.block = dict(zip(ORDER, blocks))
        self.half = blocks[0].shape[1] // 2
        self.sums = (self.block[4][:, : self.half], self.block[4][:, self.half :])
        self.left = 3

    def step(self, *values):
        up, down = (
            lax.ppermute(v.astype(BF), "fsdp", way) for v, way in zip(self.sums, self.ways)
        )
        up, down, values = pinned(up, down, values)
        up, down = up.astype(F32), down.astype(F32)
        block, half, left = self.block, self.half, self.left
        if left == 3:
            up = jnp.concatenate([block[3][:, :half] + up, block[3][:, half:]], axis=1)
            down = jnp.concatenate([block[-3][:, :half], block[-3][:, half:] + down], axis=1)
        elif left:
            up, down = block[left] + up, block[-left] + down
        self.sums = (up, down)
        self.left -= 1
        return values

    def total(self):
        while self.left >= 0:
            self.step()
        return self.block[0] + self.sums[0] + self.sums[1]


def row_ring(terms, outer):
    rows = terms.shape[0] // CHIPS
    return RingSum([terms[i * rows : (i + 1) * rows] for i in range(CHIPS)], outer)


def ring_scatter(terms, outer, beside=()):
    ring = row_ring(terms, outer)
    beside = [ring.step(value)[0] for value in beside]
    return ring.total(), beside


def ring_chips(chip):
    odd = chip & 1
    spot = (chip >> 1) * (1 - 2 * odd) + 7 * odd
    spots = [(spot + d) & 7 for d in ORDER]
    return [2 * at + (at >> 2) * (15 - 4 * at) for at in spots]


def chip_sum(terms, place, outer):
    blocks = [
        sum(lax.dynamic_index_in_dim(t, chip, 0, keepdims=False).astype(F32) for t in terms)
        for chip in ring_chips(place // 2)
    ]
    return RingSum(blocks, outer)


class Scattered:
    def __init__(self, rows):
        self.rows = rows

    def step(self, *values):
        return values

    def total(self):
        return self.rows


def section_total(value):
    for bit in range((lax.axis_size("fsdp") - 1).bit_length()):
        pairs = [(i, i ^ (1 << bit)) for i in range(lax.axis_size("fsdp"))]
        value = value + lax.ppermute(value, "fsdp", pairs)
    return value


def pinned(*values):
    return lax.optimization_barrier(values)


def layout(lengths):
    seq_ends = jnp.cumsum(lengths, axis=-1)
    offsets = jnp.arange(TOK_MB, dtype=jnp.int32)
    passed = (offsets[:, None] >= seq_ends[..., None, :]).astype(jnp.int32)
    segments = jnp.sum(passed, axis=-1)
    positions = offsets - jnp.sum(passed * lengths[..., None, :], axis=-1)
    valid = segments < lengths.shape[-1]
    return (segments, positions, valid)


def norm_rows(values, scale_gain):
    return (
        values * lax.rsqrt(jnp.mean(values * values, axis=-1, keepdims=True) + EPSILON) * scale_gain
    )


def rotate(values, positions):
    half_width = values.shape[-1] // 2
    frequency = ROPE_BASE ** (-2.0 * jnp.arange(half_width, dtype=F32) / values.shape[-1])
    angles = positions.astype(F32)[..., None, None] * frequency
    cosine = jnp.cos(angles)
    sine_part = jnp.sin(angles)
    front_half = values[..., :half_width]
    back_half = values[..., half_width:]
    return jnp.concatenate(
        [front_half * cosine - back_half * sine_part, back_half * cosine + front_half * sine_part],
        axis=-1,
    )


def forward_dot(left_array, right_array):
    return jnp.dot(left_array, right_array, preferred_element_type=F32)


def back_dot(grad_array, weight_array):
    return lax.dot_general(
        grad_array, weight_array, (((1,), (1,)), ((), ())), preferred_element_type=F32
    )


def outer_kernel(left_ref, right_ref, out_ref):
    out_ref[...] = lax.dot_general(
        left_ref[...], right_ref[...], (((0,), (0,)), ((), ())), preferred_element_type=F32
    ).astype(out_ref.dtype)


def row_outer(left_array, right_array):
    rows, height = left_array.shape
    width = right_array.shape[1]
    step = 384
    return pl.pallas_call(
        outer_kernel,
        grid=(height // step,),
        in_specs=[
            pl.BlockSpec((rows, step), lambda i: (0, i)),
            pl.BlockSpec((rows, width), lambda i: (0, 0)),
        ],
        out_specs=pl.BlockSpec((step, width), lambda i: (i, 0)),
        out_shape=jax.ShapeDtypeStruct((height, width), BF),
        compiler_params=pltpu.CompilerParams(vmem_limit_bytes=32 * 1024 * 1024),
        cost_estimate=pl.CostEstimate(
            flops=2 * rows * height * width,
            bytes_accessed=2 * (rows * height + rows * width + height * width),
            transcendentals=0,
        ),
        name="row_outer",
    )(left_array, right_array)


def split_kernel(core_ref, left_ref, right_ref, mine_ref, twin_ref, sums_ref):
    chunk = mine_ref.shape[1]
    sums_ref[...] = lax.dot_general(
        left_ref[...], right_ref[...], (((0,), (0,)), ((), ())), preferred_element_type=F32
    )
    for i in range(mine_ref.shape[0]):
        for out_ref, owner in ((mine_ref, core_ref[0]), (twin_ref, 1 - core_ref[0])):
            start = pl.multiple_of((2 * i + owner) * chunk, 8)
            out_ref[i] = sums_ref[pl.ds(start, chunk), :].astype(out_ref.dtype)


def row_outer_split(left_array, right_array, core):
    rows, height = left_array.shape
    width = right_array.shape[1]
    step = 384
    chunk = height // GROUP
    part = jax.ShapeDtypeStruct((CHIPS, chunk, width), BF)
    out_spec = pl.BlockSpec((step // chunk // 2, chunk, width), lambda i, c: (i, 0, 0))
    return pl.pallas_call(
        split_kernel,
        grid_spec=pltpu.PrefetchScalarGridSpec(
            num_scalar_prefetch=1,
            grid=(height // step,),
            in_specs=[
                pl.BlockSpec((rows, step), lambda i, c: (0, i)),
                pl.BlockSpec((rows, width), lambda i, c: (0, 0)),
            ],
            out_specs=[out_spec, out_spec],
            scratch_shapes=[pltpu.VMEM((step, width), F32)],
        ),
        out_shape=[part, part],
        compiler_params=pltpu.CompilerParams(vmem_limit_bytes=32 * 1024 * 1024),
        cost_estimate=pl.CostEstimate(
            flops=2 * rows * height * width,
            bytes_accessed=2 * (rows * height + rows * width + height * width),
            transcendentals=0,
        ),
        name="row_outer_split",
    )(core.reshape(1), left_array, right_array)


def mixer_terms_kernel(
    core_ref, normed_ref, right_ref, mixed_ref, grad_ref, mine_ref, twin_ref, in_ref, out_ref
):
    width = right_ref.shape[1]
    chunk = mine_ref.shape[1]
    half = mixed_ref.shape[1]
    step = in_ref.shape[0]
    owners = ((mine_ref, core_ref[0]), (twin_ref, 1 - core_ref[0]))
    for i in range(normed_ref.shape[1] // step):
        in_ref[...] = lax.dot_general(
            normed_ref[:, i * step : (i + 1) * step],
            right_ref[...],
            (((0,), (0,)), ((), ())),
            preferred_element_type=F32,
        )
        for j in range(step // chunk // 2):
            for part_ref, owner in owners:
                start = pl.multiple_of((2 * j + owner) * chunk, 8)
                part_ref[i * (step // chunk // 2) + j, :, :width] = in_ref[
                    pl.ds(start, chunk), :
                ].astype(BF)
    for i in range(2):
        out_ref[...] = lax.dot_general(
            mixed_ref[...],
            grad_ref[:, i * half : (i + 1) * half],
            (((0,), (0,)), ((), ())),
            preferred_element_type=F32,
        )
        for j in range(CHIPS):
            for part_ref, owner in owners:
                start = pl.multiple_of((2 * j + owner) * (chunk // 2), 8)
                part_ref[j, i * (chunk // 2) : (i + 1) * (chunk // 2), width:] = out_ref[
                    pl.ds(start, chunk // 2), :
                ].astype(BF)


def mixer_terms(normed, rights, mixed, grad_pair, core):
    rows, height = normed.shape
    width = rights.shape[1]
    half = mixed.shape[1]
    part = jax.ShapeDtypeStruct((CHIPS, height // GROUP, width + half), BF)
    whole = pl.BlockSpec(memory_space=pltpu.VMEM)
    return pl.pallas_call(
        mixer_terms_kernel,
        in_specs=[pl.BlockSpec(memory_space=pltpu.SMEM)] + [whole] * 4,
        out_specs=[whole, whole],
        out_shape=[part, part],
        scratch_shapes=[pltpu.VMEM((384, width), F32), pltpu.VMEM((half, half), F32)],
        compiler_params=pltpu.CompilerParams(vmem_limit_bytes=48 * 1024 * 1024),
        cost_estimate=pl.CostEstimate(
            flops=2 * rows * height * (width + half),
            bytes_accessed=2 * height * (width + half),
            transcendentals=0,
        ),
        name="mixer_terms",
    )(core.reshape(1), normed, rights, mixed, grad_pair)


def owned_kernel(side_ref, *refs):
    own0_ref, *came0_refs = refs[:3]
    own1_ref, *came1_refs = refs[3:6]
    width = own0_ref.shape[3]
    half = came0_refs[0].shape[0]

    def write(own_ref, came_refs, own_first):
        for i in range(CHIPS):
            for j, out_ref in enumerate(refs[6:]):
                rows = [own_ref[i, j].astype(F32), came_refs[i // half][i % half, j].astype(F32)]
                out_ref[:, i * width : (i + 1) * width] = jnp.concatenate(
                    rows if own_first else rows[::-1], axis=0
                )

    pl.when(side_ref[0] == 0)(lambda: write(own0_ref, came0_refs, True))
    pl.when(side_ref[0] == 1)(lambda: write(own1_ref, came1_refs, False))


def owned_rows(own0, came0, own1, came1, side):
    depth, width = 2 * own0.shape[2], CHIPS * own0.shape[3]
    whole = pl.BlockSpec(memory_space=pltpu.VMEM)
    return pl.pallas_call(
        owned_kernel,
        in_specs=[pl.BlockSpec(memory_space=pltpu.SMEM)] + [whole] * 6,
        out_specs=[whole] * 3,
        out_shape=[jax.ShapeDtypeStruct((depth, width), F32)] * 3,
        compiler_params=pltpu.CompilerParams(vmem_limit_bytes=48 * 1024 * 1024),
        cost_estimate=pl.CostEstimate(
            flops=0, bytes_accessed=24 * depth * width, transcendentals=0
        ),
        name="owned_rows",
    )(side.reshape(1), own0, *came0, own1, *came1)


def prepare(queries, keys_in, head_gain_pair, positions):
    return (
        rotate(norm_rows(queries, head_gain_pair[0]), positions),
        rotate(norm_rows(keys_in, head_gain_pair[1]), positions),
    )


def attention_parts(normed, first_matrix, pair_matrix, head_gain_pair, segments, positions):
    row_count = normed.shape[0]
    kv_heads = KV_HEADS // SIDES
    group_size = HEADS // KV_HEADS
    queries = forward_dot(normed, first_matrix).reshape(row_count, HEADS // SIDES, HEAD_DIM)
    key_values = forward_dot(normed, pair_matrix).reshape(row_count, 2, kv_heads, HEAD_DIM)
    queries_rot, keys_rot = prepare(queries, key_values[:, 0], head_gain_pair, positions)
    queries_low = queries_rot.astype(BF).reshape(row_count, kv_heads, group_size, HEAD_DIM)
    keys_low = keys_rot.astype(BF)
    values_low = key_values[:, 1].astype(BF)
    offsets = jnp.arange(row_count)
    allowed = (segments[:, None] == segments[None, :]) & (offsets[:, None] >= offsets[None, :])
    scale_factor = HEAD_DIM ** (-0.5)
    scores = (
        jnp.einsum("qhgd,khd->hgqk", queries_low, keys_low, preferred_element_type=F32)
        * scale_factor
    )
    scores = jnp.where(allowed, scores, MASKED_SCORE)
    probabilities = jax.nn.softmax(scores, axis=-1)
    probs_low = probabilities.astype(BF)
    mixed = jnp.einsum("hgqk,khd->qhgd", probs_low, values_low, preferred_element_type=F32)
    mixed = mixed.reshape(row_count, -1).astype(BF)
    return (
        mixed,
        (queries, key_values, queries_low, keys_low, values_low, probabilities, probs_low),
    )


def attention_back(grad_out, context, first_matrix, pair_matrix, head_gain_pair, positions):
    queries, key_values, queries_low, keys_low, values_low, probabilities, probs_low = context
    row_count = grad_out.shape[0]
    kv_heads = KV_HEADS // SIDES
    group_size = HEADS // KV_HEADS
    scale_factor = HEAD_DIM ** (-0.5)
    grad_low = grad_out.astype(BF).reshape(row_count, kv_heads, group_size, HEAD_DIM)
    grad_probs = jnp.einsum("qhgd,khd->hgqk", grad_low, values_low, preferred_element_type=F32)
    grad_values = jnp.einsum("hgqk,qhgd->khd", probs_low, grad_low, preferred_element_type=F32)
    grad_scores = probabilities * (
        grad_probs - jnp.sum(grad_probs * probabilities, axis=-1, keepdims=True)
    )
    grad_scores = grad_scores.astype(BF)
    grad_queries = (
        jnp.einsum("hgqk,khd->qhgd", grad_scores, keys_low, preferred_element_type=F32)
        * scale_factor
    )
    grad_keys = (
        jnp.einsum("hgqk,qhgd->khd", grad_scores, queries_low, preferred_element_type=F32)
        * scale_factor
    )

    def prepared(query_in, key_in, gain_in):
        return prepare(query_in, key_in, gain_in, positions)

    unused_value, pull_prep = jax.vjp(prepared, queries, key_values[:, 0], head_gain_pair)
    grad_query_pre, grad_key_pre, grad_head = pull_prep(
        (grad_queries.reshape(queries.shape), grad_keys)
    )
    grad_first = grad_query_pre.reshape(row_count, -1).astype(BF)
    grad_pairs = (
        jnp.stack([grad_key_pre, grad_values], axis=1).reshape(row_count, -1).astype(BF)
    )
    grad_normed = back_dot(grad_first, first_matrix) + back_dot(grad_pairs, pair_matrix)
    return (grad_normed, grad_first, grad_pairs, grad_head)


def conv_mix(signal, gate_pair, kernel_rows, positions):
    width = signal.shape[-1]
    carried = gate_pair[:, :width] * signal
    summed = kernel_rows[0] * carried
    for lag_steps in (1, 2):
        delayed = jnp.concatenate(
            [jnp.zeros((lag_steps, width), F32), carried[:-lag_steps]], axis=0
        )
        summed = summed + kernel_rows[lag_steps] * jnp.where(
            (positions >= lag_steps)[:, None], delayed, 0.0
        )
    return gate_pair[:, width:] * summed


def conv_parts(normed, first_matrix, gating_matrix, kernel_rows, positions):
    signal = forward_dot(normed, first_matrix)
    gate_pair = forward_dot(normed, gating_matrix)
    mixed = conv_mix(signal, gate_pair, kernel_rows, positions).astype(BF)
    return (mixed, (signal, gate_pair))


def conv_back(grad_out, context, first_matrix, gating_matrix, kernel_rows, positions):
    signal, gate_pair = context

    def mixing(signal_in, gates_in, kernel_in):
        return conv_mix(signal_in, gates_in, kernel_in, positions)

    unused_value, pull_conv = jax.vjp(mixing, signal, gate_pair, kernel_rows)
    grad_signal, grad_gates, grad_kernel = pull_conv(grad_out)
    grad_first = grad_signal.astype(BF)
    grad_gates = grad_gates.astype(BF)
    grad_normed = back_dot(grad_first, first_matrix) + back_dot(grad_gates, gating_matrix)
    return (grad_normed, grad_first, grad_gates, grad_kernel)


def glu_unit(gate_in, up_in):
    return jax.nn.silu(gate_in) * up_in


def on_device(
    section_inputs,
    seq_lengths,
    norm_gains,
    head_gains,
    conv_kernel,
    first_weight,
    out_weight,
    gate_weight,
    up_weight,
    down_weight,
    pair_weight,
    gating_weight,
):
    side = lax.axis_index("section")
    on_first = side == 0
    shards = lax.axis_size("fsdp")
    outer = shards // GROUP
    place = lax.axis_index("fsdp")
    core = place % 2
    on_core0 = core == 0
    same_core = [
        [GROUP * o + 2 * a + c for a in range(CHIPS)] for o in range(outer) for c in range(2)
    ]
    across = [[GROUP * o + i for o in range(outer)] for i in range(GROUP)]
    depth = first_weight.shape[1]
    model_width = first_weight.shape[2]
    half_width = model_width // SIDES
    pair_half = pair_weight.shape[1] // 2 // SIDES
    hidden_part = gate_weight.shape[2] // CHIPS

    def pick(first_value, second_value):
        return jnp.where(on_first, first_value, second_value)

    def half_of(columns, width):
        return lax.dynamic_slice_in_dim(columns, side * width, width, axis=1)

    def other_half_of(columns, width):
        return lax.dynamic_slice_in_dim(columns, (1 - side) * width, width, axis=1)

    rows = section_inputs[0]
    arrived = other_side(pick(rows[TOK_MB:], rows[:TOK_MB]))
    start_rows = pick(rows[:TOK_MB], arrived).astype(F32)
    cotangent = pick(arrived, rows[TOK_MB:])
    segments, positions, valid = layout(seq_lengths)
    own_valid = pick(valid[0], valid[1])[:, None]
    segments = segments + 8 * jnp.arange(2, dtype=jnp.int32)[:, None]
    segments = pick(segments.reshape(-1), segments[::-1].reshape(-1))
    positions = pick(positions.reshape(-1), positions[::-1].reshape(-1))

    first_kept = half_of(first_weight[0], half_width)
    first_came = other_side(other_half_of(first_weight[0], half_width))
    pair_own = jnp.concatenate(
        [
            half_of(pair_weight[:, : pair_half * SIDES], pair_half),
            half_of(pair_weight[:, pair_half * SIDES :], pair_half),
        ],
        axis=1,
    )
    gating_own = jnp.concatenate(
        [
            half_of(gating_weight[:, :model_width], half_width),
            half_of(gating_weight[:, model_width:], half_width),
        ],
        axis=1,
    )
    out_kept = out_weight[0].reshape(2, depth // 2, model_width)

    def out_pairs(block, part):
        sides = shards // SIDES
        return [
            (block * shards + j, (j // sides) * shards + 2 * (j % sides) + part)
            for j in range(shards)
        ]

    def out_shard(block):
        parts = [
            lax.ppermute(out_kept[part], ("section", "fsdp"), out_pairs(block, part))
            for part in range(2)
        ]
        return jnp.where(place % 2 == 0, parts[0], parts[1])

    def section_rows(matrix):
        if outer > 1:
            matrix = lax.all_gather(
                matrix, "fsdp", axis=0, tiled=True, axis_index_groups=across
            )
        return matrix

    def row_half(matrix, which):
        return lax.dynamic_slice_in_dim(
            matrix, which * (matrix.shape[0] // 2), matrix.shape[0] // 2, axis=0
        )

    def chunks(matrix):
        return matrix.reshape(-1, CHIPS, hidden_part).transpose(1, 0, 2)

    def exchanged(chunks):
        return lax.all_to_all(chunks, "fsdp", 0, 0, axis_index_groups=same_core)

    def assembled(mine, swapped):
        twin = other_core(mine, outer)
        twin_swapped = other_core(swapped, outer)
        whole = []
        for j in range(3):
            a, b, c, d = (v[:, j] for v in (mine, swapped, twin, twin_swapped))
            lower, lower_swapped = jnp.where(on_core0, a, c), jnp.where(on_core0, b, d)
            upper, upper_swapped = jnp.where(on_core0, c, a), jnp.where(on_core0, d, b)
            both = jnp.stack(
                [
                    jnp.concatenate(
                        [pick(lower, lower_swapped), pick(lower_swapped, lower)], axis=1
                    ),
                    jnp.concatenate(
                        [pick(upper, upper_swapped), pick(upper_swapped, upper)], axis=1
                    ),
                ],
                axis=1,
            )
            both = both.reshape(CHIPS, 2, outer, depth, hidden_part)
            whole.append(both.transpose(2, 0, 1, 3, 4).reshape(model_width, hidden_part))
        return whole

    def out_flat(part):
        return jnp.concatenate([part[:, :half_width], part[:, half_width:]], axis=0)

    def out_matrix(flat):
        flat = flat.reshape(shards, 2, depth // 2, half_width)
        return jnp.concatenate(
            [flat[:, i].reshape(half_width, half_width) for i in range(2)], axis=1
        )

    attention_part = jnp.concatenate(
        [pick(first_kept, first_came), pair_own, out_flat(out_shard(0))], axis=1
    )
    conv_part = jnp.concatenate(
        [pick(first_came, first_kept), gating_own, out_flat(out_shard(1))], axis=1
    )
    attention_all = lax.all_gather(attention_part, "fsdp", axis=0, tiled=True)
    matrices = [section_rows(m) for m in (gate_weight[0], up_weight[0], down_weight[0].T)]
    sent_raw, unused_first = pinned([row_half(m, 1 - side) for m in matrices], first_came)
    came_raw = [other_side(m) for m in sent_raw]
    kept_raw = [row_half(m, side) for m in matrices]
    laid0 = exchanged(
        jnp.stack([chunks(pick(k, c)) for k, c in zip(kept_raw, came_raw)], axis=1)
    )

    first_half0 = attention_all[:, :half_width]
    pair_part = attention_all[:, half_width : half_width + 2 * pair_half]
    out_half0 = out_matrix(attention_all[:, half_width + 2 * pair_half :])
    kernel_half = half_of(conv_kernel, half_width)

    def paired(own):
        return jnp.concatenate([own, other_side(own)], axis=0)

    def pair_sum(terms):
        return terms[:TOK_MB] + other_side(terms[TOK_MB:].astype(BF)).astype(F32)

    def feed_forward(all_h, mlp):
        gate_pre = forward_dot(all_h, mlp[0])
        up_pre = forward_dot(all_h, mlp[1])
        active = glu_unit(gate_pre, up_pre).astype(BF)
        return (back_dot(active, mlp[2]), (all_h, gate_pre, up_pre, active))

    def feed_back(all_up, saved, mlp):
        all_h, gate_pre, up_pre, active = saved
        grad_active = forward_dot(all_up, mlp[2])
        unused_value, pull_glu = jax.vjp(glu_unit, gate_pre, up_pre)
        grad_gate, grad_up = pull_glu(grad_active)
        grad_gate = grad_gate.astype(BF)
        grad_up = grad_up.astype(BF)
        terms = tuple(
            outer_split(left, right)
            for left, right in ((all_h, grad_gate), (all_h, grad_up), (all_up, active))
        )
        return (back_dot(grad_gate, mlp[0]) + back_dot(grad_up, mlp[1]), terms)

    def outer_split(left, right):
        if outer == 1:
            return row_outer_split(left, right, core)
        term = row_outer(left, right).astype(F32)
        term = lax.psum(term, "fsdp", axis_index_groups=across).astype(BF)
        term = term.reshape(outer, CHIPS, 2, depth, hidden_part).transpose(2, 1, 0, 3, 4)
        term = term.reshape(2, CHIPS, outer * depth, hidden_part)
        return tuple(
            lax.dynamic_index_in_dim(term, owner, 0, keepdims=False) for owner in (core, 1 - core)
        )

    def out_blocks(term):
        parts = [
            term[:, i * half_width : (i + 1) * half_width].reshape(shards, -1, half_width)
            for i in range(2)
        ]
        return jnp.concatenate(parts, axis=1).reshape(model_width, half_width)

    def out_unblocks(rows_of):
        return jnp.concatenate([rows_of[: depth // 2], rows_of[depth // 2 :]], axis=1)

    def mixer_cores(normed, rights, mixed, grad_pair):
        rights = jnp.concatenate(rights, axis=1)
        if outer == 1:
            mine, twin = mixer_terms(normed, rights, mixed, grad_pair, core)
            return mine, other_core(twin, outer)
        term = jnp.concatenate(
            [row_outer(normed, rights), out_blocks(row_outer(mixed, grad_pair))], axis=1
        )
        return lax.psum_scatter(term, "fsdp", scatter_dimension=0, tiled=True)

    def mixer_sum(cores):
        return Scattered(cores) if outer > 1 else chip_sum(cores, place, outer)

    normed0 = paired(norm_rows(start_rows, norm_gains[0, 0]).astype(BF))
    mixed0, context0 = attention_parts(
        normed0, first_half0, pair_part, head_gains, segments, positions
    )
    hidden0 = start_rows + pair_sum(forward_dot(mixed0, out_half0))
    hidden0, laid0, conv_part = pinned(hidden0, laid0, conv_part)
    swapped0 = other_side(laid0)
    conv_all = lax.all_gather(conv_part, "fsdp", axis=0, tiled=True)
    normed_h0 = norm_rows(hidden0, norm_gains[0, 1]).astype(BF)
    all_h0 = ring_gather(normed_h0, outer)
    all_h0, swapped0 = pinned(all_h0, swapped0)
    mlp0 = assembled(laid0, swapped0)
    fed_term0, saved0 = feed_forward(all_h0, mlp0)
    fed0 = row_ring(fed_term0, outer)
    fed0.step()
    fed0.step()
    (raw1,) = fed0.step([pick(c, k) for k, c in zip(kept_raw, came_raw)])
    fed0 = fed0.total()
    laid1 = exchanged(jnp.stack([chunks(m) for m in raw1], axis=1))
    middle = (hidden0 + fed0).astype(BF)

    middle_rows = middle.astype(F32)
    first_half1 = conv_all[:, :half_width]
    gating_part = conv_all[:, half_width : 3 * half_width]
    out_half1 = out_matrix(conv_all[:, 3 * half_width :])
    normed1 = paired(norm_rows(middle_rows, norm_gains[1, 0]).astype(BF))
    mixed1, context1 = conv_parts(normed1, first_half1, gating_part, kernel_half, positions)
    hidden1 = middle_rows + pair_sum(forward_dot(mixed1, out_half1))
    normed_h1 = norm_rows(hidden1, norm_gains[1, 1]).astype(BF)
    nothing = jnp.zeros_like(cotangent)
    upstream1 = jnp.where(own_valid, cotangent, nothing)
    both = ring_blocks(jnp.concatenate([normed_h1, upstream1], axis=0), outer)
    all_h1 = jnp.concatenate([part[:TOK_MB] for part in both], axis=0)
    all_up1 = jnp.concatenate([part[TOK_MB:] for part in both], axis=0)
    all_h1, all_up1, swapped1 = pinned(all_h1, all_up1, other_side(laid1))
    mlp1 = assembled(laid1, swapped1)
    fed_term1, saved1 = feed_forward(all_h1, mlp1)

    def core_sum(terms):
        return [
            (mine.astype(F32) + other_core(twin, outer).astype(F32))
            .astype(BF)
            .reshape(CHIPS, 2, -1, hidden_part)
            for mine, twin in terms
        ]

    def side_sum(terms):
        kept, sent = (
            jnp.stack(
                [lax.dynamic_index_in_dim(t, which, 1, keepdims=False) for t in terms], axis=1
            )
            for which in (side, 1 - side)
        )
        return (kept.astype(F32) + other_side(sent).astype(F32)).astype(BF)

    back_term1, terms1 = feed_back(all_up1, saved1, mlp1)
    grad_h1, terms1 = ring_scatter(back_term1, outer, terms1)
    unused_norm, pull_hidden1 = jax.vjp(norm_rows, hidden1, norm_gains[1, 1])
    grad_hidden1, gain_h1 = pull_hidden1(grad_h1)
    grad_hidden1 = grad_hidden1 + upstream1.astype(F32)
    grad_hidden1, fed_term1 = pinned(grad_hidden1, fed_term1)
    fed1 = row_ring(fed_term1, outer)
    grad_pair1, cores1 = fed1.step(paired(grad_hidden1.astype(BF)), core_sum(terms1))
    grad_normed1, grad_first1, grad_gating, grad_kernel = conv_back(
        back_dot(grad_pair1, out_half1), context1, first_half1, gating_part, kernel_half, positions
    )
    grad_normed1, grad_first1, grad_gating, grad_kernel = fed1.step(
        grad_normed1, grad_first1, grad_gating, grad_kernel
    )
    (grad_normed1,) = fed1.step(pair_sum(grad_normed1))
    grad_normed1, cores1 = pinned(grad_normed1, cores1)
    sides1 = side_sum(cores1)
    unused_norm, pull_start1 = jax.vjp(norm_rows, middle_rows, norm_gains[1, 0])
    grad_start1, gain_x1 = pull_start1(grad_normed1)
    grad_middle = (grad_start1 + grad_hidden1).astype(BF)

    all_up0 = ring_gather(grad_middle, outer)
    conv_cores = mixer_cores(normed1, [grad_first1, grad_gating], mixed1, grad_pair1)
    final = (hidden1 + fed1.total()).astype(BF)
    all_up0, conv_cores, final = pinned(all_up0, conv_cores, final)
    back_term0, terms0 = feed_back(all_up0, saved0, mlp0)
    ring = row_ring(back_term0, outer)
    terms0 = [ring.step(term)[0] for term in terms0[:2]] + [terms0[2]]
    terms0[2], sides1, conv_cores = ring.step(terms0[2], sides1, conv_cores)
    conv_sum = mixer_sum(conv_cores)
    (sides1,) = conv_sum.step(sides1)
    grad_h0 = ring.total()
    cores0 = core_sum(terms0)
    unused_norm, pull_hidden0 = jax.vjp(norm_rows, hidden0, norm_gains[0, 1])
    grad_hidden0, gain_h0 = pull_hidden0(grad_h0)
    grad_hidden0 = grad_hidden0 + grad_middle.astype(F32)
    grad_pair0, cores0 = conv_sum.step(paired(grad_hidden0.astype(BF)), cores0)
    grad_normed0, grad_first0, grad_pairs, grad_head = attention_back(
        back_dot(grad_pair0, out_half0), context0, first_half0, pair_part, head_gains, positions
    )
    grad_normed0, grad_first0, grad_pairs, grad_head = conv_sum.step(
        grad_normed0, grad_first0, grad_pairs, grad_head
    )
    (grad_normed0,) = conv_sum.step(pair_sum(grad_normed0))
    grad_normed0, cores0 = pinned(grad_normed0, cores0)
    sides0 = side_sum(cores0)
    conv_sums = conv_sum.total().astype(BF)
    conv_sums, sides1 = pinned(conv_sums, sides1)
    sent1 = exchanged(sides1)
    unused_norm, pull_start0 = jax.vjp(norm_rows, start_rows, norm_gains[0, 0])
    grad_start0, gain_x0 = pull_start0(grad_normed0)
    grad_start = (grad_start0 + grad_hidden0).astype(BF)
    kernel_whole = lax.dynamic_update_slice_in_dim(
        jnp.zeros_like(conv_kernel), grad_kernel, side * half_width, axis=1
    )
    head_row = jnp.pad(grad_head.reshape(1, -1), ((0, 0), (0, model_width - grad_head.size)))
    small = jnp.concatenate(
        [jnp.stack([gain_x0, gain_h0, gain_x1, gain_h1]), kernel_whole, head_row], axis=0
    )
    small = section_total(small)
    sides0, sent1, small = pinned(sides0, sent1, small)
    sent0 = exchanged(sides0)

    attention_cores = mixer_cores(normed0, [grad_first0, grad_pairs], mixed0, grad_pair0)

    def returned(first_rows, second_rows):
        kept = pick(first_rows, second_rows)
        came = other_side(pick(second_rows, first_rows))
        return jnp.concatenate([pick(kept, came), pick(came, kept)], axis=0)

    activation_rows = returned(
        jnp.where(own_valid, middle, nothing), jnp.where(own_valid, final, nothing)
    )
    input_rows = returned(grad_start, grad_middle)

    conv_came = other_side(conv_sums[:, : 3 * half_width])
    small = small + other_side(small)
    sent0, attention_cores, input_rows, activation_rows, conv_came, small = pinned(
        sent0, attention_cores, input_rows, activation_rows, conv_came, small
    )
    half = CHIPS // 2
    came0 = [to_side(part, 0) for part in (sent0[:half], sent0[half:])]
    came1 = [to_side(part, 1) for part in (sent1[:half], sent1[half:])]
    def owned(number):
        own = pick(sent0[:, number], sent1[:, number])
        came = pick(*(jnp.concatenate(c, axis=0)[:, number] for c in (came0, came1)))
        rows_of = jnp.concatenate([pick(own, came), pick(came, own)], axis=1)
        rows_of = rows_of.transpose(1, 0, 2).reshape(outer, depth, -1)
        return lax.dynamic_index_in_dim(rows_of, place // GROUP, 0, keepdims=False).astype(F32)

    attention_sum = mixer_sum(attention_cores)
    attention_sum.step()
    attention_sum.step()
    came0[0], came1[0] = attention_sum.step(came0[0], came1[0])
    attention_sums = attention_sum.total().astype(BF)
    attention_came = other_side(attention_sums[:, : half_width + 2 * pair_half])
    out_sums0 = out_unblocks(attention_sums[:, half_width + 2 * pair_half :])
    out_sums1 = out_unblocks(conv_sums[:, 3 * half_width :])

    even_place = place % 2 == 0
    out_sent = (
        jnp.where(even_place, out_sums0, out_sums1),
        jnp.where(even_place, out_sums1, out_sums0),
    )
    out_came = [
        lax.ppermute(
            value,
            ("section", "fsdp"),
            [(b, a) for part in range(2) for a, b in out_pairs((part + turn) % 2, part)],
        )
        for turn, value in enumerate(out_sent)
    ]
    out_rows = jnp.concatenate(
        [pick(out_came[0], out_came[1]), pick(out_came[1], out_came[0])], axis=0
    ).astype(F32)

    def both_halves(own_part, came_part):
        return jnp.concatenate([pick(own_part, came_part), pick(came_part, own_part)], axis=1)

    def columns(own, came, width, start):
        return jnp.concatenate(
            [
                both_halves(own[:, i : i + width], came[:, i : i + width])
                for i in (start, start + width)
            ],
            axis=1,
        )

    came0, came1, attention_came = pinned(came0, came1, attention_came)
    first_rows = both_halves(
        pick(attention_sums[:, :half_width], conv_sums[:, :half_width]),
        pick(attention_came[:, :half_width], conv_came[:, :half_width]),
    )
    pair_rows = columns(attention_sums, attention_came, pair_half, half_width)
    gating_rows = columns(conv_sums, conv_came, half_width, half_width)

    if outer == 1:
        grad_gate, grad_up, grad_down = owned_rows(sent0, came0, sent1, came1, side)
    else:
        grad_gate, grad_up, grad_down = (owned(number) for number in range(3))

    return (
        activation_rows[None],
        input_rows[None],
        small[:4].reshape(2, 2, model_width),
        small[7, : grad_head.size].reshape(grad_head.shape),
        small[4:7],
        first_rows.astype(F32)[None],
        out_rows[None],
        grad_gate[None],
        grad_up[None],
        grad_down.T[None],
        pair_rows.astype(F32),
        gating_rows.astype(F32),
    )


def solution(mesh):
    in_specs = (
        P("section", "fsdp", None),
        P("fsdp", None),
        P(),
        P(),
        P(),
        P("section", "fsdp", None),
        P("section", "fsdp", None),
        P("section", "fsdp", None),
        P("section", "fsdp", None),
        P("section", None, "fsdp"),
        P("fsdp", None),
        P("fsdp", None),
    )
    out_specs = (
        P("section", "fsdp", None),
        P("section", "fsdp", None),
        P(),
        P(),
        P(),
        P("section", "fsdp", None),
        P("section", "fsdp", None),
        P("section", "fsdp", None),
        P("section", "fsdp", None),
        P("section", None, "fsdp"),
        P("fsdp", None),
        P("fsdp", None),
    )
    return jax.shard_map(
        on_device, mesh=mesh, in_specs=in_specs, out_specs=out_specs, check_vma=False
    )
```

```python
import jax
import jax.numpy as jnp
from jax import lax
from jax.experimental import pallas as pl
from jax.experimental.pallas import tpu as pltpu
from jax.sharding import PartitionSpec as P

HEADS = 24
KV_HEADS = 8
HEAD_DIM = 64
TOK_MB = 64
SIDES = 2
GROUP = 16
CHIPS = 8
RING = (0, 2, 4, 6, 7, 5, 3, 1)

EPSILON = 1e-05
ROPE_BASE = 1000000.0
MASKED_SCORE = -1000000000.0

BF = jnp.bfloat16
F32 = jnp.float32


def group_pairs(chip_pairs, outer):
    return [
        (GROUP * o + 2 * a + c, GROUP * o + 2 * b + c)
        for o in range(outer)
        for a, b in chip_pairs
        for c in range(2)
    ]


def forward_ring(outer):
    return group_pairs([(RING[i], RING[(i + 1) % CHIPS]) for i in range(CHIPS)], outer)


def backward_ring(outer):
    return group_pairs([(RING[(i + 1) % CHIPS], RING[i]) for i in range(CHIPS)], outer)


def other_core(value, outer):
    return lax.ppermute(value, "fsdp", [(i, i ^ 1) for i in range(GROUP * outer)])


def other_side(value):
    return lax.ppermute(value, "section", [(0, 1), (1, 0)])


def to_side(value, side):
    return lax.ppermute(value, "section", [(1 - side, side)])


ORDER = (0, -1, 1, -2, 2, -3, 3, 4)


def ring_blocks(own, outer):
    fwd, bwd = forward_ring(outer), backward_ring(outer)
    blocks = [own]
    up, down = own, own
    for _ in range(3):
        up, down = lax.ppermute(up, "fsdp", fwd), lax.ppermute(down, "fsdp", bwd)
        blocks += [up, down]
    half = own.shape[1] // 2
    left = lax.ppermute(up[:, :half], "fsdp", fwd)
    right = lax.ppermute(down[:, half:], "fsdp", bwd)
    blocks.append(jnp.concatenate([left, right], axis=1))
    return blocks


def ring_gather(own, outer):
    return jnp.concatenate(ring_blocks(own, outer), axis=0)


class RingSum:
    def __init__(self, blocks, outer):
        self.ways = forward_ring(outer), backward_ring(outer)
        self.block = dict(zip(ORDER, blocks))
        self.half = blocks[0].shape[1] // 2
        self.sums = (self.block[4][:, : self.half], self.block[4][:, self.half :])
        self.left = 3

    def step(self, *values):
        up, down = (
            lax.ppermute(v.astype(BF), "fsdp", way) for v, way in zip(self.sums, self.ways)
        )
        up, down, values = pinned(up, down, values)
        up, down = up.astype(F32), down.astype(F32)
        block, half, left = self.block, self.half, self.left
        if left == 3:
            up = jnp.concatenate([block[3][:, :half] + up, block[3][:, half:]], axis=1)
            down = jnp.concatenate([block[-3][:, :half], block[-3][:, half:] + down], axis=1)
        elif left:
            up, down = block[left] + up, block[-left] + down
        self.sums = (up, down)
        self.left -= 1
        return values

    def total(self):
        while self.left >= 0:
            self.step()
        return self.block[0] + self.sums[0] + self.sums[1]


def row_ring(terms, outer):
    rows = terms.shape[0] // CHIPS
    return RingSum([terms[i * rows : (i + 1) * rows] for i in range(CHIPS)], outer)


def ring_scatter(terms, outer, beside=()):
    ring = row_ring(terms, outer)
    beside = [ring.step(value)[0] for value in beside]
    return ring.total(), beside


def ring_chips(chip):
    odd = chip & 1
    spot = (chip >> 1) * (1 - 2 * odd) + 7 * odd
    spots = [(spot + d) & 7 for d in ORDER]
    return [2 * at + (at >> 2) * (15 - 4 * at) for at in spots]


def chip_sum(terms, place, outer):
    blocks = [
        sum(lax.dynamic_index_in_dim(t, chip, 0, keepdims=False).astype(F32) for t in terms)
        for chip in ring_chips(place // 2)
    ]
    return RingSum(blocks, outer)


class Scattered:
    def __init__(self, rows):
        self.rows = rows

    def step(self, *values):
        return values

    def total(self):
        return self.rows


def section_total(value):
    for bit in range((lax.axis_size("fsdp") - 1).bit_length()):
        pairs = [(i, i ^ (1 << bit)) for i in range(lax.axis_size("fsdp"))]
        value = value + lax.ppermute(value, "fsdp", pairs)
    return value


def pinned(*values):
    return lax.optimization_barrier(values)


def layout(lengths):
    seq_ends = jnp.cumsum(lengths, axis=-1)
    offsets = jnp.arange(TOK_MB, dtype=jnp.int32)
    passed = (offsets[:, None] >= seq_ends[..., None, :]).astype(jnp.int32)
    segments = jnp.sum(passed, axis=-1)
    positions = offsets - jnp.sum(passed * lengths[..., None, :], axis=-1)
    valid = segments < lengths.shape[-1]
    return (segments, positions, valid)


def norm_rows(values, scale_gain):
    return (
        values * lax.rsqrt(jnp.mean(values * values, axis=-1, keepdims=True) + EPSILON) * scale_gain
    )


def rotate(values, positions):
    half_width = values.shape[-1] // 2
    frequency = ROPE_BASE ** (-2.0 * jnp.arange(half_width, dtype=F32) / values.shape[-1])
    angles = positions.astype(F32)[..., None, None] * frequency
    cosine = jnp.cos(angles)
    sine_part = jnp.sin(angles)
    front_half = values[..., :half_width]
    back_half = values[..., half_width:]
    return jnp.concatenate(
        [front_half * cosine - back_half * sine_part, back_half * cosine + front_half * sine_part],
        axis=-1,
    )


def forward_dot(left_array, right_array):
    return jnp.dot(left_array, right_array, preferred_element_type=F32)


def back_dot(grad_array, weight_array):
    return lax.dot_general(
        grad_array, weight_array, (((1,), (1,)), ((), ())), preferred_element_type=F32
    )


def outer_kernel(left_ref, right_ref, out_ref):
    out_ref[...] = lax.dot_general(
        left_ref[...], right_ref[...], (((0,), (0,)), ((), ())), preferred_element_type=F32
    ).astype(out_ref.dtype)


def row_outer(left_array, right_array):
    rows, height = left_array.shape
    width = right_array.shape[1]
    step = 384
    return pl.pallas_call(
        outer_kernel,
        grid=(height // step,),
        in_specs=[
            pl.BlockSpec((rows, step), lambda i: (0, i)),
            pl.BlockSpec((rows, width), lambda i: (0, 0)),
        ],
        out_specs=pl.BlockSpec((step, width), lambda i: (i, 0)),
        out_shape=jax.ShapeDtypeStruct((height, width), BF),
        compiler_params=pltpu.CompilerParams(vmem_limit_bytes=32 * 1024 * 1024),
        cost_estimate=pl.CostEstimate(
            flops=2 * rows * height * width,
            bytes_accessed=2 * (rows * height + rows * width + height * width),
            transcendentals=0,
        ),
        name="row_outer",
    )(left_array, right_array)


def split_kernel(core_ref, left_ref, right_ref, mine_ref, twin_ref, sums_ref):
    chunk = mine_ref.shape[1]
    sums_ref[...] = lax.dot_general(
        left_ref[...], right_ref[...], (((0,), (0,)), ((), ())), preferred_element_type=F32
    )
    for i in range(mine_ref.shape[0]):
        for out_ref, owner in ((mine_ref, core_ref[0]), (twin_ref, 1 - core_ref[0])):
            start = pl.multiple_of((2 * i + owner) * chunk, 8)
            out_ref[i] = sums_ref[pl.ds(start, chunk), :].astype(out_ref.dtype)


def row_outer_split(left_array, right_array, core):
    rows, height = left_array.shape
    width = right_array.shape[1]
    step = 384
    chunk = height // GROUP
    part = jax.ShapeDtypeStruct((CHIPS, chunk, width), BF)
    out_spec = pl.BlockSpec((step // chunk // 2, chunk, width), lambda i, c: (i, 0, 0))
    return pl.pallas_call(
        split_kernel,
        grid_spec=pltpu.PrefetchScalarGridSpec(
            num_scalar_prefetch=1,
            grid=(height // step,),
            in_specs=[
                pl.BlockSpec((rows, step), lambda i, c: (0, i)),
                pl.BlockSpec((rows, width), lambda i, c: (0, 0)),
            ],
            out_specs=[out_spec, out_spec],
            scratch_shapes=[pltpu.VMEM((step, width), F32)],
        ),
        out_shape=[part, part],
        compiler_params=pltpu.CompilerParams(vmem_limit_bytes=32 * 1024 * 1024),
        cost_estimate=pl.CostEstimate(
            flops=2 * rows * height * width,
            bytes_accessed=2 * (rows * height + rows * width + height * width),
            transcendentals=0,
        ),
        name="row_outer_split",
    )(core.reshape(1), left_array, right_array)


def mixer_terms_kernel(
    core_ref, normed_ref, right_ref, mixed_ref, grad_ref, mine_ref, twin_ref, in_ref, out_ref
):
    width = right_ref.shape[1]
    chunk = mine_ref.shape[1]
    half = mixed_ref.shape[1]
    step = in_ref.shape[0]
    owners = ((mine_ref, core_ref[0]), (twin_ref, 1 - core_ref[0]))
    for i in range(normed_ref.shape[1] // step):
        in_ref[...] = lax.dot_general(
            normed_ref[:, i * step : (i + 1) * step],
            right_ref[...],
            (((0,), (0,)), ((), ())),
            preferred_element_type=F32,
        )
        for j in range(step // chunk // 2):
            for part_ref, owner in owners:
                start = pl.multiple_of((2 * j + owner) * chunk, 8)
                part_ref[i * (step // chunk // 2) + j, :, :width] = in_ref[
                    pl.ds(start, chunk), :
                ].astype(BF)
    for i in range(2):
        out_ref[...] = lax.dot_general(
            mixed_ref[...],
            grad_ref[:, i * half : (i + 1) * half],
            (((0,), (0,)), ((), ())),
            preferred_element_type=F32,
        )
        for j in range(CHIPS):
            for part_ref, owner in owners:
                start = pl.multiple_of((2 * j + owner) * (chunk // 2), 8)
                part_ref[j, i * (chunk // 2) : (i + 1) * (chunk // 2), width:] = out_ref[
                    pl.ds(start, chunk // 2), :
                ].astype(BF)


def mixer_terms(normed, rights, mixed, grad_pair, core):
    rows, height = normed.shape
    width = rights.shape[1]
    half = mixed.shape[1]
    part = jax.ShapeDtypeStruct((CHIPS, height // GROUP, width + half), BF)
    whole = pl.BlockSpec(memory_space=pltpu.VMEM)
    return pl.pallas_call(
        mixer_terms_kernel,
        in_specs=[pl.BlockSpec(memory_space=pltpu.SMEM)] + [whole] * 4,
        out_specs=[whole, whole],
        out_shape=[part, part],
        scratch_shapes=[pltpu.VMEM((384, width), F32), pltpu.VMEM((half, half), F32)],
        compiler_params=pltpu.CompilerParams(vmem_limit_bytes=48 * 1024 * 1024),
        cost_estimate=pl.CostEstimate(
            flops=2 * rows * height * (width + half),
            bytes_accessed=2 * height * (width + half),
            transcendentals=0,
        ),
        name="mixer_terms",
    )(core.reshape(1), normed, rights, mixed, grad_pair)


def owned_kernel(side_ref, *refs):
    own0_ref, *came0_refs = refs[:3]
    own1_ref, *came1_refs = refs[3:6]
    width = own0_ref.shape[3]
    half = came0_refs[0].shape[0]

    def write(own_ref, came_refs, own_first):
        for i in range(CHIPS):
            for j, out_ref in enumerate(refs[6:]):
                rows = [own_ref[i, j].astype(F32), came_refs[i // half][i % half, j].astype(F32)]
                out_ref[:, i * width : (i + 1) * width] = jnp.concatenate(
                    rows if own_first else rows[::-1], axis=0
                )

    pl.when(side_ref[0] == 0)(lambda: write(own0_ref, came0_refs, True))
    pl.when(side_ref[0] == 1)(lambda: write(own1_ref, came1_refs, False))


def owned_rows(own0, came0, own1, came1, side):
    depth, width = 2 * own0.shape[2], CHIPS * own0.shape[3]
    whole = pl.BlockSpec(memory_space=pltpu.VMEM)
    return pl.pallas_call(
        owned_kernel,
        in_specs=[pl.BlockSpec(memory_space=pltpu.SMEM)] + [whole] * 6,
        out_specs=[whole] * 3,
        out_shape=[jax.ShapeDtypeStruct((depth, width), F32)] * 3,
        compiler_params=pltpu.CompilerParams(vmem_limit_bytes=48 * 1024 * 1024),
        cost_estimate=pl.CostEstimate(
            flops=0, bytes_accessed=24 * depth * width, transcendentals=0
        ),
        name="owned_rows",
    )(side.reshape(1), own0, *came0, own1, *came1)


def prepare(queries, keys_in, head_gain_pair, positions):
    return (
        rotate(norm_rows(queries, head_gain_pair[0]), positions),
        rotate(norm_rows(keys_in, head_gain_pair[1]), positions),
    )


def attention_parts(normed, first_matrix, pair_matrix, head_gain_pair, segments, positions):
    row_count = normed.shape[0]
    kv_heads = KV_HEADS // SIDES
    group_size = HEADS // KV_HEADS
    queries = forward_dot(normed, first_matrix).reshape(row_count, HEADS // SIDES, HEAD_DIM)
    key_values = forward_dot(normed, pair_matrix).reshape(row_count, 2, kv_heads, HEAD_DIM)
    queries_rot, keys_rot = prepare(queries, key_values[:, 0], head_gain_pair, positions)
    queries_low = queries_rot.astype(BF).reshape(row_count, kv_heads, group_size, HEAD_DIM)
    keys_low = keys_rot.astype(BF)
    values_low = key_values[:, 1].astype(BF)
    offsets = jnp.arange(row_count)
    allowed = (segments[:, None] == segments[None, :]) & (offsets[:, None] >= offsets[None, :])
    scale_factor = HEAD_DIM ** (-0.5)
    scores = (
        jnp.einsum("qhgd,khd->hgqk", queries_low, keys_low, preferred_element_type=F32)
        * scale_factor
    )
    scores = jnp.where(allowed, scores, MASKED_SCORE)
    probabilities = jax.nn.softmax(scores, axis=-1)
    probs_low = probabilities.astype(BF)
    mixed = jnp.einsum("hgqk,khd->qhgd", probs_low, values_low, preferred_element_type=F32)
    mixed = mixed.reshape(row_count, -1).astype(BF)
    return (
        mixed,
        (queries, key_values, queries_low, keys_low, values_low, probabilities, probs_low),
    )


def attention_back(grad_out, context, first_matrix, pair_matrix, head_gain_pair, positions):
    queries, key_values, queries_low, keys_low, values_low, probabilities, probs_low = context
    row_count = grad_out.shape[0]
    kv_heads = KV_HEADS // SIDES
    group_size = HEADS // KV_HEADS
    scale_factor = HEAD_DIM ** (-0.5)
    grad_low = grad_out.astype(BF).reshape(row_count, kv_heads, group_size, HEAD_DIM)
    grad_probs = jnp.einsum("qhgd,khd->hgqk", grad_low, values_low, preferred_element_type=F32)
    grad_values = jnp.einsum("hgqk,qhgd->khd", probs_low, grad_low, preferred_element_type=F32)
    grad_scores = probabilities * (
        grad_probs - jnp.sum(grad_probs * probabilities, axis=-1, keepdims=True)
    )
    grad_scores = grad_scores.astype(BF)
    grad_queries = (
        jnp.einsum("hgqk,khd->qhgd", grad_scores, keys_low, preferred_element_type=F32)
        * scale_factor
    )
    grad_keys = (
        jnp.einsum("hgqk,qhgd->khd", grad_scores, queries_low, preferred_element_type=F32)
        * scale_factor
    )

    def prepared(query_in, key_in, gain_in):
        return prepare(query_in, key_in, gain_in, positions)

    unused_value, pull_prep = jax.vjp(prepared, queries, key_values[:, 0], head_gain_pair)
    grad_query_pre, grad_key_pre, grad_head = pull_prep(
        (grad_queries.reshape(queries.shape), grad_keys)
    )
    grad_first = grad_query_pre.reshape(row_count, -1).astype(BF)
    grad_pairs = (
        jnp.stack([grad_key_pre, grad_values], axis=1).reshape(row_count, -1).astype(BF)
    )
    grad_normed = back_dot(grad_first, first_matrix) + back_dot(grad_pairs, pair_matrix)
    return (grad_normed, grad_first, grad_pairs, grad_head)


def conv_mix(signal, gate_pair, kernel_rows, positions):
    width = signal.shape[-1]
    carried = gate_pair[:, :width] * signal
    summed = kernel_rows[0] * carried
    for lag_steps in (1, 2):
        delayed = jnp.concatenate(
            [jnp.zeros((lag_steps, width), F32), carried[:-lag_steps]], axis=0
        )
        summed = summed + kernel_rows[lag_steps] * jnp.where(
            (positions >= lag_steps)[:, None], delayed, 0.0
        )
    return gate_pair[:, width:] * summed


def conv_parts(normed, first_matrix, gating_matrix, kernel_rows, positions):
    signal = forward_dot(normed, first_matrix)
    gate_pair = forward_dot(normed, gating_matrix)
    mixed = conv_mix(signal, gate_pair, kernel_rows, positions).astype(BF)
    return (mixed, (signal, gate_pair))


def conv_back(grad_out, context, first_matrix, gating_matrix, kernel_rows, positions):
    signal, gate_pair = context

    def mixing(signal_in, gates_in, kernel_in):
        return conv_mix(signal_in, gates_in, kernel_in, positions)

    unused_value, pull_conv = jax.vjp(mixing, signal, gate_pair, kernel_rows)
    grad_signal, grad_gates, grad_kernel = pull_conv(grad_out)
    grad_first = grad_signal.astype(BF)
    grad_gates = grad_gates.astype(BF)
    grad_normed = back_dot(grad_first, first_matrix) + back_dot(grad_gates, gating_matrix)
    return (grad_normed, grad_first, grad_gates, grad_kernel)


def glu_unit(gate_in, up_in):
    return jax.nn.silu(gate_in) * up_in


def on_device(
    section_inputs,
    seq_lengths,
    norm_gains,
    head_gains,
    conv_kernel,
    first_weight,
    out_weight,
    gate_weight,
    up_weight,
    down_weight,
    pair_weight,
    gating_weight,
):
    side = lax.axis_index("section")
    on_first = side == 0
    shards = lax.axis_size("fsdp")
    outer = shards // GROUP
    place = lax.axis_index("fsdp")
    core = place % 2
    on_core0 = core == 0
    same_core = [
        [GROUP * o + 2 * a + c for a in range(CHIPS)] for o in range(outer) for c in range(2)
    ]
    across = [[GROUP * o + i for o in range(outer)] for i in range(GROUP)]
    depth = first_weight.shape[1]
    model_width = first_weight.shape[2]
    half_width = model_width // SIDES
    pair_half = pair_weight.shape[1] // 2 // SIDES
    hidden_part = gate_weight.shape[2] // CHIPS

    def pick(first_value, second_value):
        return jnp.where(on_first, first_value, second_value)

    def half_of(columns, width):
        return lax.dynamic_slice_in_dim(columns, side * width, width, axis=1)

    def other_half_of(columns, width):
        return lax.dynamic_slice_in_dim(columns, (1 - side) * width, width, axis=1)

    rows = section_inputs[0]
    arrived = other_side(pick(rows[TOK_MB:], rows[:TOK_MB]))
    start_rows = pick(rows[:TOK_MB], arrived).astype(F32)
    cotangent = pick(arrived, rows[TOK_MB:])
    segments, positions, valid = layout(seq_lengths)
    own_valid = pick(valid[0], valid[1])[:, None]
    segments = segments + 8 * jnp.arange(2, dtype=jnp.int32)[:, None]
    segments = pick(segments.reshape(-1), segments[::-1].reshape(-1))
    positions = pick(positions.reshape(-1), positions[::-1].reshape(-1))

    first_kept = half_of(first_weight[0], half_width)
    first_came = other_side(other_half_of(first_weight[0], half_width))
    pair_own = jnp.concatenate(
        [
            half_of(pair_weight[:, : pair_half * SIDES], pair_half),
            half_of(pair_weight[:, pair_half * SIDES :], pair_half),
        ],
        axis=1,
    )
    gating_own = jnp.concatenate(
        [
            half_of(gating_weight[:, :model_width], half_width),
            half_of(gating_weight[:, model_width:], half_width),
        ],
        axis=1,
    )
    out_kept = out_weight[0].reshape(2, depth // 2, model_width)

    def out_pairs(block, part):
        sides = shards // SIDES
        return [
            (block * shards + j, (j // sides) * shards + 2 * (j % sides) + part)
            for j in range(shards)
        ]

    def out_shard(block, kept):
        parts = [
            lax.ppermute(kept[part], ("section", "fsdp"), out_pairs(block, part))
            for part in range(2)
        ]
        return jnp.where(place % 2 == 0, parts[0], parts[1])

    def section_rows(matrix):
        if outer > 1:
            matrix = lax.all_gather(
                matrix, "fsdp", axis=0, tiled=True, axis_index_groups=across
            )
        return matrix

    def row_half(matrix, which):
        return lax.dynamic_slice_in_dim(
            matrix, which * (matrix.shape[0] // 2), matrix.shape[0] // 2, axis=0
        )

    def chunks(matrix):
        return matrix.reshape(-1, CHIPS, hidden_part).transpose(1, 0, 2)

    def exchanged(chunks):
        return lax.all_to_all(chunks, "fsdp", 0, 0, axis_index_groups=same_core)

    def assembled(mine, swapped):
        twin = other_core(mine, outer)
        twin_swapped = other_core(swapped, outer)
        whole = []
        for j in range(3):
            a, b, c, d = (v[:, j] for v in (mine, swapped, twin, twin_swapped))
            lower, lower_swapped = jnp.where(on_core0, a, c), jnp.where(on_core0, b, d)
            upper, upper_swapped = jnp.where(on_core0, c, a), jnp.where(on_core0, d, b)
            both = jnp.stack(
                [
                    jnp.concatenate(
                        [pick(lower, lower_swapped), pick(lower_swapped, lower)], axis=1
                    ),
                    jnp.concatenate(
                        [pick(upper, upper_swapped), pick(upper_swapped, upper)], axis=1
                    ),
                ],
                axis=1,
            )
            both = both.reshape(CHIPS, 2, outer, depth, hidden_part)
            whole.append(both.transpose(2, 0, 1, 3, 4).reshape(model_width, hidden_part))
        return whole

    def out_flat(part):
        return jnp.concatenate([part[:, :half_width], part[:, half_width:]], axis=0)

    def out_matrix(flat):
        flat = flat.reshape(shards, 2, depth // 2, half_width)
        return jnp.concatenate(
            [flat[:, i].reshape(half_width, half_width) for i in range(2)], axis=1
        )

    attention_part = jnp.concatenate(
        [pick(first_kept, first_came), pair_own, out_flat(out_shard(0, out_kept))], axis=1
    )
    attention_all = lax.all_gather(attention_part, "fsdp", axis=0, tiled=True)
    matrices = [section_rows(m) for m in (gate_weight[0], up_weight[0], down_weight[0].T)]
    sent_raw, unused_first = pinned([row_half(m, 1 - side) for m in matrices], first_came)
    came_raw = [other_side(m) for m in sent_raw]
    kept_raw = [row_half(m, side) for m in matrices]
    laid0 = exchanged(
        jnp.stack([chunks(pick(k, c)) for k, c in zip(kept_raw, came_raw)], axis=1)
    )

    first_half0 = attention_all[:, :half_width]
    pair_part = attention_all[:, half_width : half_width + 2 * pair_half]
    out_half0 = out_matrix(attention_all[:, half_width + 2 * pair_half :])
    kernel_half = half_of(conv_kernel, half_width)

    def paired(own):
        return jnp.concatenate([own, other_side(own)], axis=0)

    def pair_sum(terms):
        return terms[:TOK_MB] + other_side(terms[TOK_MB:].astype(BF)).astype(F32)

    def feed_forward(all_h, mlp):
        gate_pre = forward_dot(all_h, mlp[0])
        up_pre = forward_dot(all_h, mlp[1])
        active = glu_unit(gate_pre, up_pre).astype(BF)
        return (back_dot(active, mlp[2]), (all_h, gate_pre, up_pre, active))

    def feed_back(all_up, saved, mlp):
        all_h, gate_pre, up_pre, active = saved
        grad_active = forward_dot(all_up, mlp[2])
        unused_value, pull_glu = jax.vjp(glu_unit, gate_pre, up_pre)
        grad_gate, grad_up = pull_glu(grad_active)
        grad_gate = grad_gate.astype(BF)
        grad_up = grad_up.astype(BF)
        terms = tuple(
            outer_split(left, right)
            for left, right in ((all_h, grad_gate), (all_h, grad_up), (all_up, active))
        )
        return (back_dot(grad_gate, mlp[0]) + back_dot(grad_up, mlp[1]), terms)

    def outer_split(left, right):
        if outer == 1:
            return row_outer_split(left, right, core)
        term = row_outer(left, right).astype(F32)
        term = lax.psum(term, "fsdp", axis_index_groups=across).astype(BF)
        term = term.reshape(outer, CHIPS, 2, depth, hidden_part).transpose(2, 1, 0, 3, 4)
        term = term.reshape(2, CHIPS, outer * depth, hidden_part)
        return tuple(
            lax.dynamic_index_in_dim(term, owner, 0, keepdims=False) for owner in (core, 1 - core)
        )

    def out_blocks(term):
        parts = [
            term[:, i * half_width : (i + 1) * half_width].reshape(shards, -1, half_width)
            for i in range(2)
        ]
        return jnp.concatenate(parts, axis=1).reshape(model_width, half_width)

    def out_unblocks(rows_of):
        return jnp.concatenate([rows_of[: depth // 2], rows_of[depth // 2 :]], axis=1)

    def mixer_cores(normed, rights, mixed, grad_pair):
        rights = jnp.concatenate(rights, axis=1)
        if outer == 1:
            mine, twin = mixer_terms(normed, rights, mixed, grad_pair, core)
            return mine, other_core(twin, outer)
        term = jnp.concatenate(
            [row_outer(normed, rights), out_blocks(row_outer(mixed, grad_pair))], axis=1
        )
        return lax.psum_scatter(term, "fsdp", scatter_dimension=0, tiled=True)

    def mixer_sum(cores):
        return Scattered(cores) if outer > 1 else chip_sum(cores, place, outer)

    normed0 = paired(norm_rows(start_rows, norm_gains[0, 0]).astype(BF))
    mixed0, context0 = attention_parts(
        normed0, first_half0, pair_part, head_gains, segments, positions
    )
    mixed0, out_kept = pinned(mixed0, out_kept)
    conv_part = jnp.concatenate(
        [pick(first_came, first_kept), gating_own, out_flat(out_shard(1, out_kept))], axis=1
    )
    hidden0 = start_rows + pair_sum(forward_dot(mixed0, out_half0))
    hidden0, laid0, conv_part = pinned(hidden0, laid0, conv_part)
    swapped0 = other_side(laid0)
    conv_all = lax.all_gather(conv_part, "fsdp", axis=0, tiled=True)
    normed_h0 = norm_rows(hidden0, norm_gains[0, 1]).astype(BF)
    all_h0 = ring_gather(normed_h0, outer)
    all_h0, swapped0 = pinned(all_h0, swapped0)
    mlp0 = assembled(laid0, swapped0)
    fed_term0, saved0 = feed_forward(all_h0, mlp0)
    fed0 = row_ring(fed_term0, outer)
    fed0.step()
    fed0.step()
    (raw1,) = fed0.step([pick(c, k) for k, c in zip(kept_raw, came_raw)])
    fed0 = fed0.total()
    laid1 = exchanged(jnp.stack([chunks(m) for m in raw1], axis=1))
    middle = (hidden0 + fed0).astype(BF)

    middle_rows = middle.astype(F32)
    first_half1 = conv_all[:, :half_width]
    gating_part = conv_all[:, half_width : 3 * half_width]
    out_half1 = out_matrix(conv_all[:, 3 * half_width :])
    normed1 = paired(norm_rows(middle_rows, norm_gains[1, 0]).astype(BF))
    mixed1, context1 = conv_parts(normed1, first_half1, gating_part, kernel_half, positions)
    hidden1 = middle_rows + pair_sum(forward_dot(mixed1, out_half1))
    normed_h1 = norm_rows(hidden1, norm_gains[1, 1]).astype(BF)
    nothing = jnp.zeros_like(cotangent)
    upstream1 = jnp.where(own_valid, cotangent, nothing)
    both = ring_blocks(jnp.concatenate([normed_h1, upstream1], axis=0), outer)
    all_h1 = jnp.concatenate([part[:TOK_MB] for part in both], axis=0)
    all_up1 = jnp.concatenate([part[TOK_MB:] for part in both], axis=0)
    all_h1, all_up1, swapped1 = pinned(all_h1, all_up1, other_side(laid1))
    mlp1 = assembled(laid1, swapped1)
    fed_term1, saved1 = feed_forward(all_h1, mlp1)

    def core_sum(terms):
        return [
            (mine.astype(F32) + other_core(twin, outer).astype(F32))
            .astype(BF)
            .reshape(CHIPS, 2, -1, hidden_part)
            for mine, twin in terms
        ]

    def side_sum(terms):
        kept, sent = (
            jnp.stack(
                [lax.dynamic_index_in_dim(t, which, 1, keepdims=False) for t in terms], axis=1
            )
            for which in (side, 1 - side)
        )
        return (kept.astype(F32) + other_side(sent).astype(F32)).astype(BF)

    back_term1, terms1 = feed_back(all_up1, saved1, mlp1)
    grad_h1, terms1 = ring_scatter(back_term1, outer, terms1)
    unused_norm, pull_hidden1 = jax.vjp(norm_rows, hidden1, norm_gains[1, 1])
    grad_hidden1, gain_h1 = pull_hidden1(grad_h1)
    grad_hidden1 = grad_hidden1 + upstream1.astype(F32)
    grad_hidden1, fed_term1 = pinned(grad_hidden1, fed_term1)
    fed1 = row_ring(fed_term1, outer)
    grad_pair1, cores1 = fed1.step(paired(grad_hidden1.astype(BF)), core_sum(terms1))
    grad_normed1, grad_first1, grad_gating, grad_kernel = conv_back(
        back_dot(grad_pair1, out_half1), context1, first_half1, gating_part, kernel_half, positions
    )
    grad_normed1, grad_first1, grad_gating, grad_kernel = fed1.step(
        grad_normed1, grad_first1, grad_gating, grad_kernel
    )
    (grad_normed1,) = fed1.step(pair_sum(grad_normed1))
    grad_normed1, cores1 = pinned(grad_normed1, cores1)
    sides1 = side_sum(cores1)
    unused_norm, pull_start1 = jax.vjp(norm_rows, middle_rows, norm_gains[1, 0])
    grad_start1, gain_x1 = pull_start1(grad_normed1)
    grad_middle = (grad_start1 + grad_hidden1).astype(BF)

    all_up0 = ring_gather(grad_middle, outer)
    conv_cores = mixer_cores(normed1, [grad_first1, grad_gating], mixed1, grad_pair1)
    final = (hidden1 + fed1.total()).astype(BF)
    all_up0, conv_cores, final = pinned(all_up0, conv_cores, final)
    back_term0, terms0 = feed_back(all_up0, saved0, mlp0)
    ring = row_ring(back_term0, outer)
    terms0 = [ring.step(term)[0] for term in terms0[:2]] + [terms0[2]]
    terms0[2], sides1, conv_cores = ring.step(terms0[2], sides1, conv_cores)
    conv_sum = mixer_sum(conv_cores)
    (sides1,) = conv_sum.step(sides1)
    grad_h0 = ring.total()
    cores0 = core_sum(terms0)
    unused_norm, pull_hidden0 = jax.vjp(norm_rows, hidden0, norm_gains[0, 1])
    grad_hidden0, gain_h0 = pull_hidden0(grad_h0)
    grad_hidden0 = grad_hidden0 + grad_middle.astype(F32)
    grad_pair0, cores0 = conv_sum.step(paired(grad_hidden0.astype(BF)), cores0)
    grad_normed0, grad_first0, grad_pairs, grad_head = attention_back(
        back_dot(grad_pair0, out_half0), context0, first_half0, pair_part, head_gains, positions
    )
    grad_normed0, grad_first0, grad_pairs, grad_head = conv_sum.step(
        grad_normed0, grad_first0, grad_pairs, grad_head
    )
    (grad_normed0,) = conv_sum.step(pair_sum(grad_normed0))
    grad_normed0, cores0 = pinned(grad_normed0, cores0)
    sides0 = side_sum(cores0)
    conv_sums = conv_sum.total().astype(BF)
    conv_sums, sides1 = pinned(conv_sums, sides1)
    sent1 = exchanged(sides1)
    unused_norm, pull_start0 = jax.vjp(norm_rows, start_rows, norm_gains[0, 0])
    grad_start0, gain_x0 = pull_start0(grad_normed0)
    grad_start = (grad_start0 + grad_hidden0).astype(BF)
    kernel_whole = lax.dynamic_update_slice_in_dim(
        jnp.zeros_like(conv_kernel), grad_kernel, side * half_width, axis=1
    )
    head_row = jnp.pad(grad_head.reshape(1, -1), ((0, 0), (0, model_width - grad_head.size)))
    small = jnp.concatenate(
        [jnp.stack([gain_x0, gain_h0, gain_x1, gain_h1]), kernel_whole, head_row], axis=0
    )
    small = section_total(small)
    sides0, sent1, small = pinned(sides0, sent1, small)
    sent0 = exchanged(sides0)

    attention_cores = mixer_cores(normed0, [grad_first0, grad_pairs], mixed0, grad_pair0)

    def returned(first_rows, second_rows):
        kept = pick(first_rows, second_rows)
        came = other_side(pick(second_rows, first_rows))
        return jnp.concatenate([pick(kept, came), pick(came, kept)], axis=0)

    activation_rows = returned(
        jnp.where(own_valid, middle, nothing), jnp.where(own_valid, final, nothing)
    )
    input_rows = returned(grad_start, grad_middle)

    conv_came = other_side(conv_sums[:, : 3 * half_width])
    small = small + other_side(small)
    sent0, attention_cores, input_rows, activation_rows, conv_came, small = pinned(
        sent0, attention_cores, input_rows, activation_rows, conv_came, small
    )
    half = CHIPS // 2
    came0 = [to_side(part, 0) for part in (sent0[:half], sent0[half:])]
    came1 = [to_side(part, 1) for part in (sent1[:half], sent1[half:])]
    def owned(number):
        own = pick(sent0[:, number], sent1[:, number])
        came = pick(*(jnp.concatenate(c, axis=0)[:, number] for c in (came0, came1)))
        rows_of = jnp.concatenate([pick(own, came), pick(came, own)], axis=1)
        rows_of = rows_of.transpose(1, 0, 2).reshape(outer, depth, -1)
        return lax.dynamic_index_in_dim(rows_of, place // GROUP, 0, keepdims=False).astype(F32)

    attention_sum = mixer_sum(attention_cores)
    attention_sum.step()
    attention_sum.step()
    came0[0], came1[0] = attention_sum.step(came0[0], came1[0])
    attention_sums = attention_sum.total().astype(BF)
    attention_came = other_side(attention_sums[:, : half_width + 2 * pair_half])
    out_sums0 = out_unblocks(attention_sums[:, half_width + 2 * pair_half :])
    out_sums1 = out_unblocks(conv_sums[:, 3 * half_width :])

    even_place = place % 2 == 0
    out_sent = (
        jnp.where(even_place, out_sums0, out_sums1),
        jnp.where(even_place, out_sums1, out_sums0),
    )
    out_came = [
        lax.ppermute(
            value,
            ("section", "fsdp"),
            [(b, a) for part in range(2) for a, b in out_pairs((part + turn) % 2, part)],
        )
        for turn, value in enumerate(out_sent)
    ]
    out_rows = jnp.concatenate(
        [pick(out_came[0], out_came[1]), pick(out_came[1], out_came[0])], axis=0
    ).astype(F32)

    def both_halves(own_part, came_part):
        return jnp.concatenate([pick(own_part, came_part), pick(came_part, own_part)], axis=1)

    def columns(own, came, width, start):
        return jnp.concatenate(
            [
                both_halves(own[:, i : i + width], came[:, i : i + width])
                for i in (start, start + width)
            ],
            axis=1,
        )

    came0, came1, attention_came = pinned(came0, came1, attention_came)
    first_rows = both_halves(
        pick(attention_sums[:, :half_width], conv_sums[:, :half_width]),
        pick(attention_came[:, :half_width], conv_came[:, :half_width]),
    )
    pair_rows = columns(attention_sums, attention_came, pair_half, half_width)
    gating_rows = columns(conv_sums, conv_came, half_width, half_width)

    if outer == 1:
        grad_gate, grad_up, grad_down = owned_rows(sent0, came0, sent1, came1, side)
    else:
        grad_gate, grad_up, grad_down = (owned(number) for number in range(3))

    return (
        activation_rows[None],
        input_rows[None],
        small[:4].reshape(2, 2, model_width),
        small[7, : grad_head.size].reshape(grad_head.shape),
        small[4:7],
        first_rows.astype(F32)[None],
        out_rows[None],
        grad_gate[None],
        grad_up[None],
        grad_down.T[None],
        pair_rows.astype(F32),
        gating_rows.astype(F32),
    )


def solution(mesh):
    in_specs = (
        P("section", "fsdp", None),
        P("fsdp", None),
        P(),
        P(),
        P(),
        P("section", "fsdp", None),
        P("section", "fsdp", None),
        P("section", "fsdp", None),
        P("section", "fsdp", None),
        P("section", None, "fsdp"),
        P("fsdp", None),
        P("fsdp", None),
    )
    out_specs = (
        P("section", "fsdp", None),
        P("section", "fsdp", None),
        P(),
        P(),
        P(),
        P("section", "fsdp", None),
        P("section", "fsdp", None),
        P("section", "fsdp", None),
        P("section", "fsdp", None),
        P("section", None, "fsdp"),
        P("fsdp", None),
        P("fsdp", None),
    )
    return jax.shard_map(
        on_device, mesh=mesh, in_specs=in_specs, out_specs=out_specs, check_vma=False
    )
```
